512 devices in a mesh: section: 2 (over x_hi), tp: 8 (over z), cp: 32 (over y, x_lo, core).
Axes of the slice: x: 4 (x_hi: 2, x_lo: 2; x = x_hi * 2 + x_lo), y: 8, z: 8, core: 2. Of those that a mesh axis runs over, the one named last changes fastest.
Arguments:
- query_rows: bfloat16 [2, 4096, 6144], P('section', 'cp', 'tp'), may hold values from -5 to 5
- key_rows: bfloat16 [2, 4096, 1024], P('section', 'cp', 'tp'), may hold values from -5 to 5
- stored_value_rows: bfloat16 [2, 4096, 1024], P('section', 'cp', 'tp'), may hold values from -6 to 6
- output_grad: bfloat16 [2, 4096, 6144], P('section', 'cp', 'tp'), may hold values from -0.75 to 0.75
- span_order: int32 [64], replicated, may hold values from 0 to 63, each once
- episode_ids: int32 [2, 4096], P('section'), may hold values from 0 to 3, never falling along the last dimension, each value on 1 to 2048 neighbouring positions
Outputs:
- query_gradient: bfloat16 [2, 4096, 6144], P('section', 'cp', 'tp')
- key_gradient: bfloat16 [2, 4096, 1024], P('section', 'cp', 'tp')
- value_gradient: bfloat16 [2, 4096, 1024], P('section', 'cp', 'tp')
The draws below stay inside these ranges and needn't reach their ends.
Inputs may be any that keep to these rules, and one draw needn't show every extreme that they name: `span_order`: each number of 0 to 63 appears once. `episode_ids`: never falls along the positions of a micro-batch; an episode covers at most 2048 positions.
All inputs are finite; a program needn't handle non-finite values.
Results may differ from the reference program's by a relative error of at most 0.018.
Values may be sent and summed in bfloat16 or wider, within the bound.
No kernel may reach another device: no remote copies, remote signals or barrier semaphores. Data moves between devices by JAX's collectives and lax.ppermute only.
A program may use at most 64 MiB of HBM per device.

```python
import math
import jax
import jax.numpy as jnp
import numpy as np
from jax import lax

QUERY_HEAD_COUNT = 48
KEY_VALUE_HEADS = 8
HEAD_SIZE = 128
TOK_DEV = 128
BATCH_TOKENS = 4096
N_CP = 32


def draw_query_rows(key, part):
    key = jax.random.fold_in(key, 11)
    base_offset = jax.random.truncated_normal(key, -5.0, 5.0, (2, BATCH_TOKENS, QUERY_HEAD_COUNT * HEAD_SIZE))
    return base_offset.astype(jnp.bfloat16)


def draw_key_rows(key, part):
    key = jax.random.fold_in(key, 23)
    base_offset = jax.random.truncated_normal(key, -5.0, 5.0, (2, BATCH_TOKENS, KEY_VALUE_HEADS * HEAD_SIZE))
    return base_offset.astype(jnp.bfloat16)


def steps_of(key, shape, shards, least, top_value):
    factor_of = 1.0
    for axis_at, parts in shards:
        steps = jax.random.uniform(jax.random.fold_in(jax.random.fold_in(key, 6), axis_at), (parts,), jnp.float32, least / len(shards), top_value / len(shards))
        factor_of = factor_of * jnp.repeat(jnp.exp(steps), shape[axis_at] // parts).reshape((-1,) + (1,) * (len(shape) - 1 - axis_at))
    return factor_of


def profile(count, total, bound, lean):
    weights = [(1 << 20) // math.isqrt(standing ** lean) + 1 for standing in range(2, count + 1)]
    rest, holding = total - bound - (count - 1), [1] * (count - 1)
    while rest > 0:
        candidates = [i for i in range(count - 1) if holding[i] < bound]
        whole, budget = sum([weights[i] for i in candidates]), rest
        for i in candidates:
            addition = min(bound - holding[i], max(1, budget * weights[i] // whole), rest)
            holding[i] = holding[i] + addition
            rest = rest - addition
    return np.array([bound] + holding)


def uneven(rng, count, total, most, skew):
    if count == 2:
        one = jax.random.randint(rng, (), max(1, total - most), min(most, total - 1) + 1)
        return jnp.stack([one, total - one])
    tallies = jnp.asarray(profile(count, total, most, skew), jnp.int32)
    couples = (count - 1) // 2
    source_of, taker = tallies[1:1 + 2 * couples:2], tallies[2:2 + 2 * couples:2]
    room = jnp.minimum(source_of - 1, most - taker)
    passed = jax.random.randint(jax.random.fold_in(rng, 1), (couples,), 0, 1 << 20) % (room + 1)
    tallies = tallies.at[1:1 + 2 * couples:2].set(source_of - passed).at[2:2 + 2 * couples:2].set(taker + passed)
    return tallies[jax.random.permutation(jax.random.fold_in(rng, 2), count)]


def centred(rng, dims, scale, most, pieces=(), kind=jnp.bfloat16):
    array = jax.random.normal(rng, dims, jnp.float32) * scale
    if len(pieces) > 0:
        array = steps_of(rng, dims, pieces, -0.22, 0.18) * array
    return jnp.clip(array, min=-most, max=most).astype(kind)


def setup_inputs(seed: int = 0) -> dict:
    splits = jax.random.split(jax.random.key(seed), 7)
    return {
        "query_rows": draw_query_rows(jax.random.fold_in(splits[6], 71), 0),
        "key_rows": draw_key_rows(jax.random.fold_in(splits[6], 71), 0),
        "stored_value_rows": centred(splits[2], (2, BATCH_TOKENS, KEY_VALUE_HEADS * HEAD_SIZE), 1.0, 6.0, ((0, 2), (1, 32), (2, 8))),
        "output_grad": centred(splits[3], (2, BATCH_TOKENS, QUERY_HEAD_COUNT * HEAD_SIZE), 0.125, 0.75, ((0, 2), (1, 32), (2, 8))),
        "span_order": jax.random.permutation(splits[4], 2 * N_CP).astype(jnp.int32),
        "episode_ids": jax.vmap(lambda own: jnp.searchsorted(jnp.cumsum(uneven(own, 4, BATCH_TOKENS, BATCH_TOKENS // 2, 0)), jnp.arange(BATCH_TOKENS), side="right"))(jax.random.split(splits[5], 2)).reshape((2, BATCH_TOKENS)).astype(jnp.int32),
    }


def span_positions(span_order, row_start, row_count, span_len):
    row_ids = row_start + jnp.arange(row_count, dtype=jnp.int32)
    slot_ids = row_ids // span_len
    matches = slot_ids[:, None] == jnp.arange(span_order.shape[0], dtype=jnp.int32)[None, :]
    span_ids = jnp.sum(jnp.where(matches, span_order[None, :], 0), axis=1)
    return (span_ids * span_len + row_ids % span_len).astype(jnp.int32)


def reference(query_rows, key_rows, stored_value_rows, output_grad, span_order, episode_ids):
    span_len = TOK_DEV // 2
    heads_per_group = QUERY_HEAD_COUNT // KEY_VALUE_HEADS
    scaling = HEAD_SIZE ** -0.5
    positions = span_positions(span_order, 0, BATCH_TOKENS, span_len)

    def one_batch(operands):
        queries, keys, values, grads, episode = operands
        seg = jnp.take(episode, positions)
        visible = (positions[None, :] <= positions[:, None]) & (seg[None, :] == seg[:, None])

        def single_head_group(group_index):
            key_head = lax.dynamic_slice_in_dim(keys, group_index * HEAD_SIZE, HEAD_SIZE, 1).astype(jnp.float32)
            value_head = lax.dynamic_slice_in_dim(values, group_index * HEAD_SIZE, HEAD_SIZE, 1).astype(jnp.float32)
            query_parts = []
            key_gradient = jnp.zeros((BATCH_TOKENS, HEAD_SIZE), jnp.float32)
            value_gradient = jnp.zeros((BATCH_TOKENS, HEAD_SIZE), jnp.float32)
            for member in range(heads_per_group):
                column = (group_index * heads_per_group + member) * HEAD_SIZE
                query_head = lax.dynamic_slice_in_dim(queries, column, HEAD_SIZE, 1).astype(jnp.float32)
                grad_head = lax.dynamic_slice_in_dim(grads, column, HEAD_SIZE, 1).astype(jnp.float32)
                scores = jnp.dot(query_head, key_head.T, preferred_element_type=jnp.float32) * scaling
                row_max = jnp.max(jnp.where(visible, scores, -jnp.inf), axis=1, keepdims=True)
                weights = jnp.where(visible, jnp.exp(scores - row_max), 0.0)
                log_total = row_max + jnp.log(jnp.sum(weights, axis=1, keepdims=True))
                probs = jnp.where(visible, jnp.exp(scores - log_total), 0.0)
                prob_grad = jnp.dot(grad_head, value_head.T, preferred_element_type=jnp.float32)
                deltas = jnp.sum(probs * prob_grad, axis=1, keepdims=True)
                score_grad = (probs * (prob_grad - deltas)).astype(jnp.bfloat16).astype(jnp.float32)
                probs_low = probs.astype(jnp.bfloat16).astype(jnp.float32)
                query_parts.append(jnp.dot(score_grad, key_head, preferred_element_type=jnp.float32) * scaling)
                key_gradient = key_gradient + jnp.dot(score_grad.T, query_head, preferred_element_type=jnp.float32) * scaling
                value_gradient = value_gradient + jnp.dot(probs_low.T, grad_head, preferred_element_type=jnp.float32)
            query_gradient = jnp.concatenate(query_parts, axis=1)
            return query_gradient.astype(jnp.bfloat16), key_gradient.astype(jnp.bfloat16), value_gradient.astype(jnp.bfloat16)

        query_gradient, key_gradient, value_gradient = lax.map(single_head_group, jnp.arange(KEY_VALUE_HEADS, dtype=jnp.int32))
        query_gradient = jnp.transpose(query_gradient, (1, 0, 2)).reshape(BATCH_TOKENS, QUERY_HEAD_COUNT * HEAD_SIZE)
        key_gradient = jnp.transpose(key_gradient, (1, 0, 2)).reshape(BATCH_TOKENS, KEY_VALUE_HEADS * HEAD_SIZE)
        value_gradient = jnp.transpose(value_gradient, (1, 0, 2)).reshape(BATCH_TOKENS, KEY_VALUE_HEADS * HEAD_SIZE)
        return query_gradient, key_gradient, value_gradient

    query_gradient, key_gradient, value_gradient = lax.map(one_batch, (query_rows, key_rows, stored_value_rows, output_grad, episode_ids))
    return jnp.roll(query_gradient, -1, axis=0), jnp.roll(key_gradient, -1, axis=0), jnp.roll(value_gradient, -1, axis=0)
```

```python
import functools

import jax
import jax.numpy as jnp
from jax import lax
from jax.experimental import pallas as pl
from jax.experimental.pallas import tpu as pltpu
from jax.sharding import Mesh
from jax.sharding import PartitionSpec as P

HEAD = 128
SPAN = 64
HEADS = 6
ROWS = HEADS * SPAN
GROUP = 4
SCALING = HEAD ** (-0.5)
LOG2E = 1.4426950408889634
NEG_FILL = -1e30
FAR = 1 << 20
NT = (((1,), (1,)), ((), ()))
NN = (((1,), (0,)), ((), ()))


def dot(a, b, dims):
    return lax.dot_general(a, b, dims, preferred_element_type=jnp.float32)


def episode_starts(episode_ref):
    ids = episode_ref[...]
    return [jnp.sum((ids < v).astype(jnp.int32)) for v in (1, 2, 3)]


def start_of(starts, pos):
    first = jnp.zeros_like(pos)
    for s in starts:
        first = jnp.maximum(first, jnp.where(s <= pos, s, 0))
    return first


def list_visible(order_ref, place_ref, starts, query_base, list_ref):
    xl, core, key_count = place_ref[1], place_ref[2], 16
    first = jnp.int32(0)
    for s in starts:
        first = jnp.maximum(first, jnp.where(s <= query_base, s, 0))
    count = jnp.int32(0)
    for k in range(key_count):
        base = order_ref[((k // 2) * 4 + xl * 2 + core) * 2 + k % 2] * SPAN
        list_ref[0, count] = k
        list_ref[1, count] = base
        seen = (base <= query_base) & (base + (SPAN - 1) >= first)
        count = count + seen.astype(jnp.int32)
    for extra in range(GROUP):
        list_ref[0, count + extra] = 0
        list_ref[1, count + extra] = FAR
    return count


def load_group(kv_ref, list_ref, step):
    spans = [list_ref[0, step * GROUP + i] for i in range(GROUP)]
    keys = jnp.concatenate([kv_ref[s, :, :HEAD] for s in spans], axis=0)
    values = jnp.concatenate([kv_ref[s, :, HEAD:] for s in spans], axis=0)
    iota = lax.broadcasted_iota(jnp.int32, (SPAN, HEAD), 0)
    pos = jnp.concatenate([list_ref[1, step * GROUP + i] + iota for i in range(GROUP)], axis=0)
    return spans, keys, values, pos


def by_rows(ref, row, column):
    return jnp.concatenate(
        [
            ref[pl.ds(row, SPAN), column + h * HEAD : column + (h + 1) * HEAD]
            for h in range(HEADS)
        ],
        axis=0,
    )


def masked_scores(scores, visible):
    return jnp.concatenate(
        [
            jnp.where(visible, scores[:, g * HEAD : (g + 1) * HEAD] * (SCALING * LOG2E), NEG_FILL)
            for g in range(ROWS // HEAD)
        ],
        axis=1,
    )


def query_spans(order_ref, place_ref, body):
    y, xl = place_ref[0], place_ref[1]
    for rel in range(2):
        chip = xl if rel == 0 else 1 - xl

        def one(i, unused, rel=rel, chip=chip):
            base = order_ref[y * 8 + chip * 4 + i] * SPAN
            body(rel, i, chip * 4 + i, base)
            return unused

        lax.fori_loop(0, 4, one, 0)


def stats_kernel(order_ref, place_ref, episode_ref, kv_ref, own_ref, other_ref, out_ref, list_ref):
    starts = episode_starts(episode_ref)
    lane = lax.broadcasted_iota(jnp.int32, (1, HEAD), 1) % SPAN

    def body(rel, i, slot, base):
        ref = (own_ref, other_ref)[rel]
        row = pl.multiple_of(i * SPAN, SPAN)
        query = by_rows(ref, row, 0)
        grad = by_rows(ref, row, HEADS * HEAD)
        query_pos = base + lane
        first = start_of(starts, query_pos)
        count = list_visible(order_ref, place_ref, starts, base, list_ref)

        def step(j, carried):
            top, total, weighted = carried
            unused, keys, values, pos = load_group(kv_ref, list_ref, j)
            visible = (pos <= query_pos) & (pos >= first)
            scores = masked_scores(dot(keys, query, NT), visible)
            products = dot(values, grad, NT)
            new_top = jnp.maximum(top, jnp.max(scores, axis=0, keepdims=True))
            weights = jnp.exp2(scores - new_top)
            keep = jnp.exp2(top - new_top)
            total = total * keep + jnp.sum(weights, axis=0, keepdims=True)
            weighted = weighted * keep + jnp.sum(weights * products, axis=0, keepdims=True)
            return new_top, total, weighted

        zero = jnp.zeros((1, ROWS), jnp.float32)
        top, total, weighted = lax.fori_loop(
            0, (count + (GROUP - 1)) // GROUP, step, (zero + NEG_FILL, zero, zero)
        )
        out_ref[pl.ds(slot, 1), :] = top
        out_ref[pl.ds(8 + slot, 1), :] = total
        out_ref[pl.ds(16 + slot, 1), :] = weighted

    query_spans(order_ref, place_ref, body)


def grads_kernel(
    order_ref,
    place_ref,
    episode_ref,
    kv_ref,
    own_ref,
    other_ref,
    stats_ref,
    keep_ref,
    send_ref,
    dkv_ref,
    list_ref,
    log_ref,
    delta_ref,
    acc_ref,
    dq_ref,
):
    starts = episode_starts(episode_ref)
    lane = lax.broadcasted_iota(jnp.int32, (1, HEAD), 1) % SPAN
    parts = stats_ref.shape[0]
    tops = [stats_ref[p, 0:8] for p in range(parts)]
    top = functools.reduce(jnp.maximum, tops)
    shares = [jnp.exp2(t - top) for t in tops]
    total = sum(stats_ref[p, 8:16] * shares[p] for p in range(parts))
    log_ref[...] = top + jnp.log2(total)
    delta_ref[...] = sum(stats_ref[p, 16:24] * shares[p] for p in range(parts)) / total
    acc_ref[...] = jnp.zeros_like(acc_ref)
    my_core = place_ref[2]

    def body(rel, i, slot, base):
        ref = (own_ref, other_ref)[rel]
        row = pl.multiple_of(i * SPAN, SPAN)
        query = by_rows(ref, row, 0)
        grad = by_rows(ref, row, HEADS * HEAD)
        query_pos = base + lane
        first = start_of(starts, query_pos)
        count = list_visible(order_ref, place_ref, starts, base, list_ref)
        log_total = log_ref[pl.ds(slot, 1), :]
        delta = delta_ref[pl.ds(slot, 1), :]
        dq_ref[...] = jnp.zeros_like(dq_ref)

        def step(j, unused):
            spans, keys, values, pos = load_group(kv_ref, list_ref, j)
            visible = (pos <= query_pos) & (pos >= first)
            scores = masked_scores(dot(keys, query, NT), visible)
            products = dot(values, grad, NT)
            probs = jnp.exp2(scores - log_total)
            score_grad = (probs * (products - delta)).astype(jnp.bfloat16)
            dq_ref[...] += dot(keys.T, score_grad, NN)
            dk = dot(score_grad, query, NN)
            dv = dot(probs.astype(jnp.bfloat16), grad, NN)
            for n in range(GROUP):
                acc_ref[spans[n], :, :HEAD] += dk[n * SPAN : (n + 1) * SPAN]
                acc_ref[spans[n], :, HEAD:] += dv[n * SPAN : (n + 1) * SPAN]
            return unused

        lax.fori_loop(0, (count + (GROUP - 1)) // GROUP, step, 0)
        out = dq_ref[...].T * SCALING
        half = pl.multiple_of((i % 2) * SPAN, SPAN)
        mine = i // 2 == my_core

        @pl.when(mine)
        def _():
            for h in range(HEADS):
                keep_ref[rel, pl.ds(half, SPAN), h * HEAD : (h + 1) * HEAD] = out[
                    h * SPAN : (h + 1) * SPAN
                ]

        @pl.when(jnp.logical_not(mine))
        def _():
            for h in range(HEADS):
                send_ref[rel, pl.ds(half, SPAN), h * HEAD : (h + 1) * HEAD] = out[
                    h * SPAN : (h + 1) * SPAN
                ].astype(jnp.bfloat16)

    query_spans(order_ref, place_ref, body)
    dkv_ref[:, :, :HEAD] = (acc_ref[:, :, :HEAD] * SCALING).astype(jnp.bfloat16)
    dkv_ref[:, :, HEAD:] = acc_ref[:, :, HEAD:].astype(jnp.bfloat16)


def swap(block, axis):
    return lax.ppermute(block, axis, [(0, 1), (1, 0)])


def per_device(query_rows, key_rows, stored_value_rows, output_grad, span_order, episode_ids):
    tokens = query_rows.shape[1]
    columns = HEADS * HEAD
    ring = lax.axis_size("y")
    place = jnp.stack([lax.axis_index("y"), lax.axis_index("xl"), lax.axis_index("core")]).astype(
        jnp.int32
    )
    both = jnp.concatenate([query_rows[0], output_grad[0]], axis=1)
    own = lax.all_gather(both, "core", axis=0, tiled=True)
    other = swap(own, "xl")
    kv = jnp.concatenate([key_rows[0], stored_value_rows[0]], axis=1)
    kv_all = lax.all_to_all(
        jnp.broadcast_to(kv[None], (ring, tokens, 2 * HEAD)), "y", 0, 0, tiled=True
    ).reshape(ring * 2, SPAN, 2 * HEAD)

    smem = pl.BlockSpec(memory_space=pltpu.SMEM)
    vmem = pl.BlockSpec(memory_space=pltpu.VMEM)
    params = pltpu.CompilerParams(vmem_limit_bytes=40 * 1024 * 1024)
    stats = pl.pallas_call(
        stats_kernel,
        out_shape=jax.ShapeDtypeStruct((24, ROWS), jnp.float32),
        in_specs=[smem, smem, vmem, vmem, vmem, vmem],
        out_specs=vmem,
        scratch_shapes=[pltpu.SMEM((2, 16 + GROUP), jnp.int32)],
        compiler_params=params,
        name="row_stats",
    )(span_order, place, episode_ids, kv_all, own, other)
    stats_all = lax.all_gather(stats, ("xl", "core"), axis=0)
    keep, send, dkv = pl.pallas_call(
        grads_kernel,
        out_shape=(
            jax.ShapeDtypeStruct((2, tokens, columns), jnp.float32),
            jax.ShapeDtypeStruct((2, tokens, columns), jnp.bfloat16),
            jax.ShapeDtypeStruct((ring * 2, SPAN, 2 * HEAD), jnp.bfloat16),
        ),
        in_specs=[smem, smem, vmem, vmem, vmem, vmem, vmem],
        out_specs=(vmem, vmem, vmem),
        scratch_shapes=[
            pltpu.SMEM((2, 16 + GROUP), jnp.int32),
            pltpu.VMEM((8, ROWS), jnp.float32),
            pltpu.VMEM((8, ROWS), jnp.float32),
            pltpu.VMEM((ring * 2, SPAN, 2 * HEAD), jnp.float32),
            pltpu.VMEM((HEAD, ROWS), jnp.float32),
        ],
        compiler_params=params,
        name="gradients",
    )(span_order, place, episode_ids, kv_all, own, other, stats_all)

    dq = keep + swap(send, "core").astype(jnp.float32)
    dq_other = swap(dq[1].astype(jnp.bfloat16), "xl")
    dkv_parts = lax.all_to_all(dkv.reshape(ring, tokens, 2 * HEAD), "y", 0, 0, tiled=True)
    dkv_sum = jnp.sum(dkv_parts.astype(jnp.float32), axis=0)
    dq_sum = dq[0] + dq_other.astype(jnp.float32)
    done = jnp.concatenate([dq_sum, dkv_sum], axis=1).astype(jnp.bfloat16)
    back = swap(done, "section")[None]
    return (
        back[:, :, :columns],
        back[:, :, columns : columns + HEAD],
        back[:, :, columns + HEAD :],
    )


def solution(mesh):
    devices = mesh.devices
    fine = Mesh(
        devices.reshape(devices.shape[0], devices.shape[1], devices.shape[2] // 4, 2, 2),
        ("section", "tp", "y", "xl", "core"),
    )
    rows = P("section", ("y", "xl", "core"), "tp")
    return jax.shard_map(
        per_device,
        mesh=fine,
        in_specs=(rows, rows, rows, rows, P(), P("section", None)),
        out_specs=(rows, rows, rows),
        check_vma=False,
    )
```

```python
import functools

import jax
import jax.numpy as jnp
from jax import lax
from jax.experimental import pallas as pl
from jax.experimental.pallas import tpu as pltpu
from jax.sharding import Mesh
from jax.sharding import PartitionSpec as P

HEAD = 128
SPAN = 64
HEADS = 6
ROWS = HEADS * SPAN
SLOTS = 8
KEYS = 16
GROUP = 4
UNROLL = 2
CHUNKS = KEYS // GROUP
STEPS = SLOTS * CHUNKS + UNROLL
SCALING = HEAD ** (-0.5)
LOG2E = 1.4426950408889634
NEG_FILL = -1e30
FAR = 1 << 20
NT = (((1,), (1,)), ((), ()))
NN = (((1,), (0,)), ((), ()))

SLOT = 16
CHUNK = SLOT + STEPS
BASE = CHUNK + STEPS
SPANS = BASE + STEPS
PLACES = SPANS + STEPS * GROUP
TABLE = PLACES + STEPS * GROUP


def dot(a, b, dims):
    return lax.dot_general(a, b, dims, preferred_element_type=jnp.float32)


def start_of(starts, pos):
    first = jnp.zeros_like(pos)
    for s in starts:
        first = jnp.maximum(first, jnp.where(s <= pos, s, 0))
    return first


def prepare_kernel(order_ref, place_ref, episode_ref, own_ref, other_ref, table_ref, q_ref, g_ref):
    y, xl, core = place_ref[0], place_ref[1], place_ref[2]
    ids = episode_ref[...]
    starts = [jnp.sum((ids < v).astype(jnp.int32)) for v in (1, 2, 3)]
    for n, s in enumerate(starts):
        table_ref[1 + n] = s
    key_bases = [
        order_ref[((k // 2) * 4 + xl * 2 + core) * 2 + k % 2] * SPAN for k in range(KEYS)
    ]

    def list_slot(slot, step):
        base = order_ref[y * SLOTS + slot] * SPAN
        first = start_of(starts, base)
        at = step * GROUP
        for k in range(KEYS):
            table_ref[SPANS + at] = k
            table_ref[PLACES + at] = key_bases[k]
            seen = (key_bases[k] <= base) & (key_bases[k] + (SPAN - 1) >= first)
            at = at + seen.astype(jnp.int32)
        count = (at - step * GROUP + GROUP - 1) // GROUP
        for extra in range(GROUP):
            table_ref[SPANS + at + extra] = 0
            table_ref[PLACES + at + extra] = FAR
        for c in range(CHUNKS):
            table_ref[SLOT + step + c] = slot
            table_ref[CHUNK + step + c] = c
            table_ref[BASE + step + c] = base
        return step + count

    steps = lax.fori_loop(0, SLOTS, list_slot, jnp.int32(0))
    for extra in range(UNROLL):
        table_ref[SLOT + steps + extra] = 0
        table_ref[CHUNK + steps + extra] = CHUNKS
        table_ref[BASE + steps + extra] = 0
        for n in range(GROUP):
            table_ref[SPANS + (steps + extra) * GROUP + n] = 0
            table_ref[PLACES + (steps + extra) * GROUP + n] = FAR
    table_ref[0] = (steps + UNROLL - 1) // UNROLL

    for rel, ref in enumerate((own_ref, other_ref)):
        chip = xl if rel == 0 else 1 - xl
        for i in range(SLOTS // 2):
            for h in range(HEADS):
                rows, cols = slice(i * SPAN, (i + 1) * SPAN), slice(h * HEAD, (h + 1) * HEAD)
                out = pl.ds(h * SPAN, SPAN)
                q_ref[chip * 4 + i, out, :] = ref[rows, cols]
                g_ref[chip * 4 + i, out, :] = ref[rows, h * HEAD + HEADS * HEAD : (h + 1 + HEADS) * HEAD]


def load_step(table_ref, kv_ref, q_ref, g_ref, step):
    slot, base = table_ref[SLOT + step], table_ref[BASE + step]
    spans = [table_ref[SPANS + step * GROUP + i] for i in range(GROUP)]
    keys = jnp.concatenate([kv_ref[s, :, :HEAD] for s in spans], axis=0)
    values = jnp.concatenate([kv_ref[s, :, HEAD:] for s in spans], axis=0)
    iota = lax.broadcasted_iota(jnp.int32, (SPAN, HEAD), 0)
    pos = jnp.concatenate(
        [table_ref[PLACES + step * GROUP + i] + iota for i in range(GROUP)], axis=0
    )
    query_pos = base + lax.broadcasted_iota(jnp.int32, (1, HEAD), 1) % SPAN
    first = start_of([table_ref[1 + n] for n in range(3)], query_pos)
    visible = (pos <= query_pos) & (pos >= first)
    query, grad = q_ref[slot], g_ref[slot]
    raw = dot(keys, query, NT)
    scores = jnp.concatenate(
        [
            jnp.where(visible, raw[:, g * HEAD : (g + 1) * HEAD] * (SCALING * LOG2E), NEG_FILL)
            for g in range(ROWS // HEAD)
        ],
        axis=1,
    )
    return slot, spans, keys, query, grad, scores, dot(values, grad, NT)


def run_steps(table_ref, one_step):
    def some(n, unused):
        for u in range(UNROLL):
            one_step(n * UNROLL + u)
        return unused

    lax.fori_loop(0, table_ref[0], some, 0)


def stats_kernel(table_ref, kv_ref, q_ref, g_ref, out_ref, top_ref, total_ref, weighted_ref):
    top_ref[...] = jnp.full_like(top_ref, NEG_FILL)
    total_ref[...] = jnp.zeros_like(total_ref)
    weighted_ref[...] = jnp.zeros_like(weighted_ref)

    def one_step(step):
        slot, spans, keys, query, grad, scores, products = load_step(
            table_ref, kv_ref, q_ref, g_ref, step
        )
        chunk = table_ref[CHUNK + step]
        top = jnp.max(scores, axis=0, keepdims=True)
        weights = jnp.exp2(scores - top)
        row = pl.ds(slot, 1)
        top_ref[chunk, row, :] = top
        total_ref[chunk, row, :] = jnp.sum(weights, axis=0, keepdims=True)
        weighted_ref[chunk, row, :] = jnp.sum(weights * products, axis=0, keepdims=True)

    run_steps(table_ref, one_step)
    parts = range(CHUNKS)
    top = functools.reduce(jnp.maximum, [top_ref[c] for c in parts])
    shares = [jnp.exp2(top_ref[c] - top) for c in parts]
    out_ref[0:8] = top
    out_ref[8:16] = sum(total_ref[c] * shares[c] for c in parts)
    out_ref[16:24] = sum(weighted_ref[c] * shares[c] for c in parts)


def step_gradients(table_ref, kv_ref, q_ref, g_ref, rows_ref, step):
    slot, spans, keys, query, grad, scores, products = load_step(
        table_ref, kv_ref, q_ref, g_ref, step
    )
    probs = jnp.exp2(scores - rows_ref[pl.ds(slot, 1), :])
    score_grad = (probs * (products - rows_ref[pl.ds(8 + slot, 1), :])).astype(jnp.bfloat16)
    return slot, spans, keys, query, grad, probs, score_grad


def key_value_kernel(table_ref, kv_ref, q_ref, g_ref, stats_ref, dkv_ref, rows_ref, acc_ref):
    parts = range(stats_ref.shape[0])
    top = functools.reduce(jnp.maximum, [stats_ref[p, 0:8] for p in parts])
    shares = [jnp.exp2(stats_ref[p, 0:8] - top) for p in parts]
    total = sum(stats_ref[p, 8:16] * shares[p] for p in parts)
    rows_ref[0:8] = top + jnp.log2(total)
    rows_ref[8:16] = sum(stats_ref[p, 16:24] * shares[p] for p in parts) / total
    acc_ref[...] = jnp.zeros_like(acc_ref)

    def one_step(step):
        slot, spans, keys, query, grad, probs, score_grad = step_gradients(
            table_ref, kv_ref, q_ref, g_ref, rows_ref, step
        )
        dk = dot(score_grad, query, NN)
        dv = dot(probs.astype(jnp.bfloat16), grad, NN)
        for n in range(GROUP):
            acc_ref[spans[n], :, :HEAD] += dk[n * SPAN : (n + 1) * SPAN]
            acc_ref[spans[n], :, HEAD:] += dv[n * SPAN : (n + 1) * SPAN]

    run_steps(table_ref, one_step)
    dkv_ref[:, :, :HEAD] = (acc_ref[:, :, :HEAD] * SCALING).astype(jnp.bfloat16)
    dkv_ref[:, :, HEAD:] = acc_ref[:, :, HEAD:].astype(jnp.bfloat16)


def query_kernel(
    place_ref, table_ref, kv_ref, q_ref, g_ref, rows_ref, after_ref, keep_ref, send_ref, acc_ref
):
    acc_ref[...] = jnp.zeros_like(acc_ref)

    def one_step(step):
        slot, spans, keys, query, grad, probs, score_grad = step_gradients(
            table_ref, kv_ref, q_ref, g_ref, rows_ref, step
        )
        acc_ref[slot] += dot(keys.T, score_grad, NN)

    run_steps(table_ref, one_step)
    xl, core = place_ref[1], place_ref[2]
    for rel in range(2):
        chip = xl if rel == 0 else 1 - xl
        for half in range(2):
            rows = slice(half * SPAN, (half + 1) * SPAN)
            mine = acc_ref[chip * 4 + core * 2 + half].T * SCALING
            theirs = acc_ref[chip * 4 + (1 - core) * 2 + half].T * SCALING
            for h in range(HEADS):
                cols, at = slice(h * HEAD, (h + 1) * HEAD), slice(h * SPAN, (h + 1) * SPAN)
                keep_ref[rel, rows, cols] = mine[at]
                send_ref[rel, rows, cols] = theirs[at].astype(jnp.bfloat16)


def swap(block, axis):
    return lax.ppermute(block, axis, [(0, 1), (1, 0)])


def per_device(query_rows, key_rows, stored_value_rows, output_grad, span_order, episode_ids):
    tokens = query_rows.shape[1]
    columns = HEADS * HEAD
    ring = lax.axis_size("y")
    place = jnp.stack([lax.axis_index("y"), lax.axis_index("xl"), lax.axis_index("core")]).astype(
        jnp.int32
    )
    copies = [jnp.broadcast_to(a, (ring, tokens, HEAD)) for a in (key_rows, stored_value_rows)]
    kv_all = lax.all_to_all(jnp.concatenate(copies, axis=2), "y", 0, 0, tiled=True).reshape(
        KEYS, SPAN, 2 * HEAD
    )
    both = jnp.concatenate([query_rows[0], output_grad[0]], axis=1)
    remote = swap(both, "xl")
    own = lax.all_gather(both, "core", axis=0, tiled=True)
    other = lax.all_gather(remote, "core", axis=0, tiled=True)

    smem = pl.BlockSpec(memory_space=pltpu.SMEM)
    vmem = pl.BlockSpec(memory_space=pltpu.VMEM)
    params = pltpu.CompilerParams(vmem_limit_bytes=40 * 1024 * 1024)
    rows_bf16 = jax.ShapeDtypeStruct((SLOTS, ROWS, HEAD), jnp.bfloat16)
    table, q, g = pl.pallas_call(
        prepare_kernel,
        out_shape=(jax.ShapeDtypeStruct((TABLE,), jnp.int32), rows_bf16, rows_bf16),
        in_specs=[smem, smem, vmem, vmem, vmem],
        out_specs=(smem, vmem, vmem),
        compiler_params=params,
        name="prepare",
    )(span_order, place, episode_ids, own, other)
    stats = pl.pallas_call(
        stats_kernel,
        out_shape=jax.ShapeDtypeStruct((24, ROWS), jnp.float32),
        in_specs=[smem, vmem, vmem, vmem],
        out_specs=vmem,
        scratch_shapes=[pltpu.VMEM((CHUNKS + 1, SLOTS, ROWS), jnp.float32)] * 3,
        compiler_params=params,
        name="row_stats",
    )(table, kv_all, q, g)
    stats_all = lax.all_gather(stats, ("xl", "core"), axis=0)
    dkv, rows = pl.pallas_call(
        key_value_kernel,
        out_shape=(
            jax.ShapeDtypeStruct((KEYS, SPAN, 2 * HEAD), jnp.bfloat16),
            jax.ShapeDtypeStruct((16, ROWS), jnp.float32),
        ),
        in_specs=[smem, vmem, vmem, vmem, vmem],
        out_specs=(vmem, vmem),
        scratch_shapes=[pltpu.VMEM((KEYS, SPAN, 2 * HEAD), jnp.float32)],
        compiler_params=params,
        name="key_value_gradients",
    )(table, kv_all, q, g, stats_all)
    dkv_parts = lax.all_to_all(dkv.reshape(ring, tokens, 2 * HEAD), "y", 0, 0, tiled=True)
    keep, send = pl.pallas_call(
        query_kernel,
        out_shape=(
            jax.ShapeDtypeStruct((2, tokens, columns), jnp.float32),
            jax.ShapeDtypeStruct((2, tokens, columns), jnp.bfloat16),
        ),
        in_specs=[smem, smem, vmem, vmem, vmem, vmem, pl.BlockSpec(memory_space=pl.ANY)],
        out_specs=(vmem, vmem),
        scratch_shapes=[pltpu.VMEM((SLOTS, HEAD, ROWS), jnp.float32)],
        compiler_params=params,
        name="query_gradients",
    )(place, table, kv_all, q, g, rows, dkv)
    sent = lax.all_gather(send, "core", axis=0)
    dq = keep + lax.dynamic_index_in_dim(sent, 1 - place[2], 0, False).astype(jnp.float32)
    parts = dq.astype(jnp.bfloat16)
    across = lax.ppermute(parts[1], ("section", "xl"), [(0, 3), (1, 2), (2, 1), (3, 0)])
    straight = swap(parts[0], "section")
    dq_back = (straight.astype(jnp.float32) + across.astype(jnp.float32)).astype(jnp.bfloat16)
    dkv_sum = jnp.sum(dkv_parts.astype(jnp.float32), axis=0).astype(jnp.bfloat16)
    dkv_back = swap(dkv_sum, "section")
    return (dq_back[None], dkv_back[None, :, :HEAD], dkv_back[None, :, HEAD:])


def solution(mesh):
    devices = mesh.devices
    fine = Mesh(
        devices.reshape(devices.shape[0], devices.shape[1], devices.shape[2] // 4, 2, 2),
        ("section", "tp", "y", "xl", "core"),
    )
    rows = P("section", ("y", "xl", "core"), "tp")
    return jax.shard_map(
        per_device,
        mesh=fine,
        in_specs=(rows, rows, rows, rows, P(), P("section", None)),
        out_specs=(rows, rows, rows),
        check_vma=False,
    )
```

```python
import functools

import jax
import jax.numpy as jnp
from jax import lax
from jax.experimental import pallas as pl
from jax.experimental.pallas import tpu as pltpu
from jax.sharding import Mesh
from jax.sharding import PartitionSpec as P

HEAD = 128
SPAN = 64
HEADS = 6
ROWS = HEADS * SPAN
SLOTS = 8
KEYS = 16
GROUP = 4
UNROLL = 4
CHUNKS = KEYS // GROUP
STEPS = SLOTS * CHUNKS + CHUNKS
SCALING = HEAD ** (-0.5)
LOG2E = 1.4426950408889634
NEG_FILL = -1e30
FAR = 1 << 20
NT = (((1,), (1,)), ((), ()))
NN = (((1,), (0,)), ((), ()))

SLOT = 16
CHUNK = SLOT + STEPS
BASE = CHUNK + STEPS
SPANS = BASE + STEPS
PLACES = SPANS + STEPS * GROUP
TABLE = PLACES + STEPS * GROUP


def dot(a, b, dims):
    return lax.dot_general(a, b, dims, preferred_element_type=jnp.float32)


def start_of(starts, pos):
    first = jnp.zeros_like(pos)
    for s in starts:
        first = jnp.maximum(first, jnp.where(s <= pos, s, 0))
    return first


def prepare_kernel(
    order_ref, place_ref, episode_ref, own_ref, table_ref, q_ref, g_ref
):
    y, xl, core = place_ref[0], place_ref[1], place_ref[2]
    ids = episode_ref[...]
    starts = [jnp.sum((ids < v).astype(jnp.int32)) for v in (1, 2, 3)]
    for n, s in enumerate(starts):
        table_ref[1 + n] = s
    key_bases = [
        order_ref[((k // 2) * 4 + xl * 2 + core) * 2 + k % 2] * SPAN for k in range(KEYS)
    ]

    def list_slot(slot, step):
        base = order_ref[y * SLOTS + slot] * SPAN
        first = start_of(starts, base)
        at = step * GROUP
        for k in range(KEYS):
            table_ref[SPANS + at] = k
            table_ref[PLACES + at] = key_bases[k]
            seen = (key_bases[k] <= base) & (key_bases[k] + (SPAN - 1) >= first)
            at = at + seen.astype(jnp.int32)
        count = (at - step * GROUP + GROUP - 1) // GROUP
        for extra in range(GROUP):
            table_ref[SPANS + at + extra] = 0
            table_ref[PLACES + at + extra] = FAR
        for c in range(CHUNKS):
            table_ref[SLOT + step + c] = slot
            table_ref[CHUNK + step + c] = c
            table_ref[BASE + step + c] = base
        return step + count

    table_ref[0] = lax.fori_loop(0, SLOTS, list_slot, jnp.int32(0))
    lay_out(own_ref, q_ref, g_ref, xl)


def lay_out(ref, q_ref, g_ref, chip):
    for n, out_ref in enumerate((q_ref, g_ref)):
        for i in range(SLOTS // 2):
            for h in range(HEADS):
                out_ref[chip * 4 + i, h * SPAN : (h + 1) * SPAN, :] = ref[
                    i * SPAN : (i + 1) * SPAN, (n * HEADS + h) * HEAD : (n * HEADS + h + 1) * HEAD
                ]


def load_step(table_ref, kv_ref, q_ref, g_ref, step):
    slot, base = table_ref[SLOT + step], table_ref[BASE + step]
    spans = [table_ref[SPANS + step * GROUP + i] for i in range(GROUP)]
    keys = jnp.concatenate([kv_ref[s, :, :HEAD] for s in spans], axis=0)
    values = jnp.concatenate([kv_ref[s, :, HEAD:] for s in spans], axis=0)
    iota = lax.broadcasted_iota(jnp.int32, (SPAN, HEAD), 0)
    pos = jnp.concatenate(
        [table_ref[PLACES + step * GROUP + i] + iota for i in range(GROUP)], axis=0
    )
    query_pos = base + lax.broadcasted_iota(jnp.int32, (1, HEAD), 1) % SPAN
    first = start_of([table_ref[1 + n] for n in range(3)], query_pos)
    visible = (pos <= query_pos) & (pos >= first)
    query, grad = q_ref[slot], g_ref[slot]
    raw = dot(keys, query, NT)
    scores = jnp.concatenate(
        [
            jnp.where(visible, raw[:, g * HEAD : (g + 1) * HEAD] * (SCALING * LOG2E), NEG_FILL)
            for g in range(ROWS // HEAD)
        ],
        axis=1,
    )
    return slot, spans, keys, query, grad, scores, dot(values, grad, NT)


def run_steps(table_ref, one_step):
    def some(n, unused):
        for u in range(UNROLL):
            one_step(n * UNROLL + u)
        return unused

    count = table_ref[0]
    whole = count // UNROLL
    lax.fori_loop(0, whole, some, 0)
    lax.fori_loop(whole * UNROLL, count, lambda step, unused: (one_step(step), unused)[1], 0)


def stats_kernel(
    place_ref,
    table_ref,
    kv_ref,
    other_ref,
    q_in_ref,
    g_in_ref,
    q_ref,
    g_ref,
    out_ref,
    top_ref,
    total_ref,
    weighted_ref,
):
    lay_out(other_ref, q_ref, g_ref, 1 - place_ref[1])
    top_ref[...] = jnp.full_like(top_ref, NEG_FILL)
    total_ref[...] = jnp.zeros_like(total_ref)
    weighted_ref[...] = jnp.zeros_like(weighted_ref)

    def one_step(step):
        slot, spans, keys, query, grad, scores, products = load_step(
            table_ref, kv_ref, q_ref, g_ref, step
        )
        chunk = table_ref[CHUNK + step]
        top = jnp.max(scores, axis=0, keepdims=True)
        weights = jnp.exp2(scores - top)
        row = pl.ds(slot, 1)
        top_ref[chunk, row, :] = top
        total_ref[chunk, row, :] = jnp.sum(weights, axis=0, keepdims=True)
        weighted_ref[chunk, row, :] = jnp.sum(weights * products, axis=0, keepdims=True)

    run_steps(table_ref, one_step)
    parts = range(CHUNKS)
    top = functools.reduce(jnp.maximum, [top_ref[c] for c in parts])
    shares = [jnp.exp2(top_ref[c] - top) for c in parts]
    out_ref[0:8] = top
    out_ref[8:16] = sum(total_ref[c] * shares[c] for c in parts)
    out_ref[16:24] = sum(weighted_ref[c] * shares[c] for c in parts)


def step_gradients(table_ref, kv_ref, q_ref, g_ref, rows_ref, step):
    slot, spans, keys, query, grad, scores, products = load_step(
        table_ref, kv_ref, q_ref, g_ref, step
    )
    probs = jnp.exp2(scores - rows_ref[pl.ds(slot, 1), :])
    score_grad = (probs * (products - rows_ref[pl.ds(8 + slot, 1), :])).astype(jnp.bfloat16)
    return slot, spans, keys, query, grad, probs, score_grad


def key_value_kernel(table_ref, kv_ref, q_ref, g_ref, stats_ref, dkv_ref, rows_ref, acc_ref):
    parts = range(stats_ref.shape[0])
    top = functools.reduce(jnp.maximum, [stats_ref[p, 0:8] for p in parts])
    shares = [jnp.exp2(stats_ref[p, 0:8] - top) for p in parts]
    total = sum(stats_ref[p, 8:16] * shares[p] for p in parts)
    rows_ref[0:8] = top + jnp.log2(total)
    rows_ref[8:16] = sum(stats_ref[p, 16:24] * shares[p] for p in parts) / total
    acc_ref[...] = jnp.zeros_like(acc_ref)

    def one_step(step):
        slot, spans, keys, query, grad, probs, score_grad = step_gradients(
            table_ref, kv_ref, q_ref, g_ref, rows_ref, step
        )
        dk = dot(score_grad, query, NN)
        dv = dot(probs.astype(jnp.bfloat16), grad, NN)
        for n in range(GROUP):
            acc_ref[spans[n], :, :HEAD] += dk[n * SPAN : (n + 1) * SPAN]
            acc_ref[spans[n], :, HEAD:] += dv[n * SPAN : (n + 1) * SPAN]

    run_steps(table_ref, one_step)
    dkv_ref[:, :, :HEAD] = (acc_ref[:, :, :HEAD] * SCALING).astype(jnp.bfloat16)
    dkv_ref[:, :, HEAD:] = acc_ref[:, :, HEAD:].astype(jnp.bfloat16)


def query_kernel(
    place_ref, table_ref, kv_ref, q_ref, g_ref, rows_ref, after_ref, keep_ref, send_ref, acc_ref
):
    acc_ref[...] = jnp.zeros_like(acc_ref)

    def one_step(step):
        slot, spans, keys, query, grad, probs, score_grad = step_gradients(
            table_ref, kv_ref, q_ref, g_ref, rows_ref, step
        )
        acc_ref[slot] += dot(keys.T, score_grad, NN)

    run_steps(table_ref, one_step)
    xl, core = place_ref[1], place_ref[2]
    for rel in range(2):
        chip = xl if rel == 0 else 1 - xl
        for half in range(2):
            rows = slice(half * SPAN, (half + 1) * SPAN)
            mine = acc_ref[chip * 4 + core * 2 + half].T * SCALING
            theirs = acc_ref[chip * 4 + (1 - core) * 2 + half].T * SCALING
            for h in range(HEADS):
                cols, at = slice(h * HEAD, (h + 1) * HEAD), slice(h * SPAN, (h + 1) * SPAN)
                keep_ref[rel, rows, cols] = mine[at]
                send_ref[rel, rows, cols] = theirs[at].astype(jnp.bfloat16)


def swap(block, axis):
    return lax.ppermute(block, axis, [(0, 1), (1, 0)])


def call(kernel, name, out_shape, in_specs, out_specs, scratch=(), aliases={}):
    return pl.pallas_call(
        kernel,
        out_shape=out_shape,
        in_specs=in_specs,
        out_specs=out_specs,
        scratch_shapes=scratch,
        input_output_aliases=aliases,
        compiler_params=pltpu.CompilerParams(vmem_limit_bytes=40 * 1024 * 1024),
        name=name,
    )


SMEM = pl.BlockSpec(memory_space=pltpu.SMEM)
VMEM = pl.BlockSpec(memory_space=pltpu.VMEM)


LAID_OUT = jax.ShapeDtypeStruct((SLOTS, ROWS, HEAD), jnp.bfloat16)


def prepare(order, place, episodes, own):
    return call(
        prepare_kernel,
        "prepare",
        (jax.ShapeDtypeStruct((TABLE,), jnp.int32), LAID_OUT, LAID_OUT),
        [SMEM, SMEM, VMEM, VMEM],
        (SMEM, VMEM, VMEM),
    )(order, place, episodes, own)


def row_stats(place, table, kv_all, other, q, g):
    return call(
        stats_kernel,
        "row_stats",
        (LAID_OUT, LAID_OUT, jax.ShapeDtypeStruct((24, ROWS), jnp.float32)),
        [SMEM, SMEM, VMEM, VMEM, VMEM, VMEM],
        (VMEM, VMEM, VMEM),
        [pltpu.VMEM((CHUNKS, SLOTS, ROWS), jnp.float32)] * 3,
        {4: 0, 5: 1},
    )(place, table, kv_all, other, q, g)


def key_value_gradients(table, kv_all, q, g, stats_all):
    return call(
        key_value_kernel,
        "key_value_gradients",
        (
            jax.ShapeDtypeStruct((KEYS, SPAN, 2 * HEAD), jnp.bfloat16),
            jax.ShapeDtypeStruct((16, ROWS), jnp.float32),
        ),
        [SMEM, VMEM, VMEM, VMEM, VMEM],
        (VMEM, VMEM),
        [pltpu.VMEM((KEYS, SPAN, 2 * HEAD), jnp.float32)],
    )(table, kv_all, q, g, stats_all)


def query_gradients(place, table, kv_all, q, g, rows, after):
    shape = (2, 2 * SPAN, HEADS * HEAD)
    return call(
        query_kernel,
        "query_gradients",
        (
            jax.ShapeDtypeStruct(shape, jnp.float32),
            jax.ShapeDtypeStruct(shape, jnp.bfloat16),
        ),
        [SMEM, SMEM, VMEM, VMEM, VMEM, VMEM, pl.BlockSpec(memory_space=pl.ANY)],
        (VMEM, VMEM),
        [pltpu.VMEM((SLOTS, HEAD, ROWS), jnp.float32)],
    )(place, table, kv_all, q, g, rows, after)


def per_device(query_rows, key_rows, stored_value_rows, output_grad, span_order, episode_ids):
    tokens = query_rows.shape[1]
    ring = lax.axis_size("y")
    place = jnp.stack([lax.axis_index("y"), lax.axis_index("xl"), lax.axis_index("core")]).astype(
        jnp.int32
    )
    kv = jnp.concatenate([key_rows[0], stored_value_rows[0]], axis=1)
    kv_all = lax.all_to_all(
        jnp.broadcast_to(kv[None], (ring, tokens, 2 * HEAD)), "y", 0, 0, tiled=True
    ).reshape(KEYS, SPAN, 2 * HEAD)
    both = jnp.concatenate([query_rows[0], output_grad[0]], axis=1)
    remote = swap(both, "xl")
    own = lax.all_gather(both, "core", axis=0, tiled=True)
    other = lax.all_gather(remote, "core", axis=0, tiled=True)
    table, q, g = prepare(span_order, place, episode_ids, own)
    q, g, stats = row_stats(place, table, kv_all, other, q, g)
    stats_all = lax.all_gather(stats, ("xl", "core"), axis=0)
    dkv, rows = key_value_gradients(table, kv_all, q, g, stats_all)
    dkv_parts = lax.all_to_all(dkv.reshape(ring, tokens, 2 * HEAD), "y", 0, 0, tiled=True)
    keep, send = query_gradients(place, table, kv_all, q, g, rows, dkv)
    sent = lax.all_gather(send, "core", axis=0)
    dq = keep + lax.dynamic_index_in_dim(sent, 1 - place[2], 0, False).astype(jnp.float32)
    parts = dq.astype(jnp.bfloat16)
    straight = swap(parts[0], "section")
    across = lax.ppermute(parts[1], ("section", "xl"), [(0, 3), (1, 2), (2, 1), (3, 0)])
    dq_back = (straight.astype(jnp.float32) + across.astype(jnp.float32)).astype(jnp.bfloat16)
    dkv_sum = jnp.sum(dkv_parts.astype(jnp.float32), axis=0).astype(jnp.bfloat16)
    dkv_back = swap(dkv_sum, "section")
    return (dq_back[None], dkv_back[None, :, :HEAD], dkv_back[None, :, HEAD:])


def solution(mesh):
    devices = mesh.devices
    fine = Mesh(
        devices.reshape(devices.shape[0], devices.shape[1], devices.shape[2] // 4, 2, 2),
        ("section", "tp", "y", "xl", "core"),
    )
    rows = P("section", ("y", "xl", "core"), "tp")
    return jax.shard_map(
        per_device,
        mesh=fine,
        in_specs=(rows, rows, rows, rows, P(), P("section", None)),
        out_specs=(rows, rows, rows),
        check_vma=False,
    )
```

```python
import functools

import jax
import jax.numpy as jnp
from jax import lax
from jax.experimental import pallas as pl
from jax.experimental.pallas import tpu as pltpu
from jax.sharding import Mesh
from jax.sharding import PartitionSpec as P

HEAD = 128
SPAN = 64
HEADS = 6
ROWS = HEADS * SPAN
SLOTS = 8
KEYS = 16
GROUP = 4
UNROLLS = (8, 4, 2, 1)
CHUNKS = KEYS // GROUP
STEPS = SLOTS * CHUNKS + CHUNKS
SCALING = HEAD ** (-0.5)
LOG2E = 1.4426950408889634
NEG_FILL = -1e30
FAR = 1 << 20
NT = (((1,), (1,)), ((), ()))
NN = (((1,), (0,)), ((), ()))

SLOT = 16
CHUNK = SLOT + STEPS
BASE = CHUNK + STEPS
SPANS = BASE + STEPS
PLACES = SPANS + STEPS * GROUP
TABLE = PLACES + STEPS * GROUP


def dot(a, b, dims):
    return lax.dot_general(a, b, dims, preferred_element_type=jnp.float32)


def start_of(starts, pos):
    first = jnp.zeros_like(pos)
    for s in starts:
        first = jnp.maximum(first, jnp.where(s <= pos, s, 0))
    return first


def prepare_kernel(
    order_ref, place_ref, episode_ref, own_ref, table_ref, q_ref, g_ref
):
    y, xl, core = place_ref[0], place_ref[1], place_ref[2]
    ids = episode_ref[...]
    starts = [jnp.sum((ids < v).astype(jnp.int32)) for v in (1, 2, 3)]
    for n, s in enumerate(starts):
        table_ref[1 + n] = s
    key_bases = [
        order_ref[((k // 2) * 4 + xl * 2 + core) * 2 + k % 2] * SPAN for k in range(KEYS)
    ]

    def list_slot(slot, step):
        base = order_ref[y * SLOTS + slot] * SPAN
        first = start_of(starts, base)
        at = step * GROUP
        for k in range(KEYS):
            table_ref[SPANS + at] = (k // 2) * 4 + k % 2
            table_ref[PLACES + at] = key_bases[k]
            seen = (key_bases[k] <= base) & (key_bases[k] + (SPAN - 1) >= first)
            at = at + seen.astype(jnp.int32)
        count = (at - step * GROUP + GROUP - 1) // GROUP
        for extra in range(GROUP):
            table_ref[SPANS + at + extra] = 0
            table_ref[PLACES + at + extra] = FAR
        for c in range(CHUNKS):
            table_ref[SLOT + step + c] = slot
            table_ref[CHUNK + step + c] = c
            table_ref[BASE + step + c] = base
        return step + count

    table_ref[0] = lax.fori_loop(0, SLOTS, list_slot, jnp.int32(0))
    lay_out(own_ref, q_ref, g_ref, xl)


def lay_out(ref, q_ref, g_ref, chip):
    for n, out_ref in enumerate((q_ref, g_ref)):
        for i in range(SLOTS // 2):
            for h in range(HEADS):
                out_ref[chip * 4 + i, h * SPAN : (h + 1) * SPAN, :] = ref[
                    i * SPAN : (i + 1) * SPAN, (n * HEADS + h) * HEAD : (n * HEADS + h + 1) * HEAD
                ]


def load_keys(table_ref, kv_ref, step):
    spans = [table_ref[SPANS + step * GROUP + i] for i in range(GROUP)]
    keys = jnp.concatenate([kv_ref[s] for s in spans], axis=0)
    values = jnp.concatenate([kv_ref[s + 2] for s in spans], axis=0)
    return spans, keys, values


def load_step(table_ref, kv_ref, q_ref, g_ref, step):
    slot, base = table_ref[SLOT + step], table_ref[BASE + step]
    spans, keys, values = load_keys(table_ref, kv_ref, step)
    iota = lax.broadcasted_iota(jnp.int32, (SPAN, HEAD), 0)
    pos = jnp.concatenate(
        [table_ref[PLACES + step * GROUP + i] + iota for i in range(GROUP)], axis=0
    )
    query_pos = base + lax.broadcasted_iota(jnp.int32, (1, HEAD), 1) % SPAN
    first = start_of([table_ref[1 + n] for n in range(3)], query_pos)
    visible = (pos <= query_pos) & (pos >= first)
    query, grad = q_ref[slot], g_ref[slot]
    raw = dot(keys, query, NT)
    scores = jnp.concatenate(
        [
            jnp.where(visible, raw[:, g * HEAD : (g + 1) * HEAD] * (SCALING * LOG2E), NEG_FILL)
            for g in range(ROWS // HEAD)
        ],
        axis=1,
    )
    return slot, spans, keys, query, grad, scores, dot(values, grad, NT)


def run_steps(table_ref, one_step):
    at, count = jnp.int32(0), table_ref[0]
    for steps in UNROLLS:

        def some(n, unused, at=at, steps=steps):
            for i in range(steps):
                one_step(at + n * steps + i)
            return unused

        turns = (count - at) // steps
        lax.fori_loop(0, turns, some, 0)
        at = at + turns * steps


def stats_kernel(
    place_ref,
    table_ref,
    kv_ref,
    other_ref,
    q_in_ref,
    g_in_ref,
    q_ref,
    g_ref,
    out_ref,
    top_ref,
    total_ref,
    weighted_ref,
):
    lay_out(other_ref, q_ref, g_ref, 1 - place_ref[1])
    top_ref[...] = jnp.full_like(top_ref, NEG_FILL)
    total_ref[...] = jnp.zeros_like(total_ref)
    weighted_ref[...] = jnp.zeros_like(weighted_ref)

    def one_step(step):
        slot, spans, keys, query, grad, scores, products = load_step(
            table_ref, kv_ref, q_ref, g_ref, step
        )
        chunk = table_ref[CHUNK + step]
        top = jnp.max(scores, axis=0, keepdims=True)
        weights = jnp.exp2(scores - top)
        row = pl.ds(slot, 1)
        top_ref[chunk, row, :] = top
        total_ref[chunk, row, :] = jnp.sum(weights, axis=0, keepdims=True)
        weighted_ref[chunk, row, :] = jnp.sum(weights * products, axis=0, keepdims=True)

    run_steps(table_ref, one_step)
    parts = range(CHUNKS)
    top = functools.reduce(jnp.maximum, [top_ref[c] for c in parts])
    shares = [jnp.exp2(top_ref[c] - top) for c in parts]
    out_ref[0:8] = top
    out_ref[8:16] = sum(total_ref[c] * shares[c] for c in parts)
    out_ref[16:24] = sum(weighted_ref[c] * shares[c] for c in parts)


def step_gradients(table_ref, kv_ref, q_ref, g_ref, rows_ref, step):
    slot, spans, keys, query, grad, scores, products = load_step(
        table_ref, kv_ref, q_ref, g_ref, step
    )
    probs = jnp.exp2(scores - rows_ref[pl.ds(slot, 1), :])
    score_grad = (probs * (products - rows_ref[pl.ds(8 + slot, 1), :])).astype(jnp.bfloat16)
    return slot, spans, keys, query, grad, probs, score_grad


def key_value_kernel(table_ref, kv_ref, q_ref, g_ref, stats_ref, dkv_ref, rows_ref, acc_ref):
    parts = range(stats_ref.shape[0])
    top = functools.reduce(jnp.maximum, [stats_ref[p, 0:8] for p in parts])
    shares = [jnp.exp2(stats_ref[p, 0:8] - top) for p in parts]
    total = sum(stats_ref[p, 8:16] * shares[p] for p in parts)
    rows_ref[0:8] = top + jnp.log2(total)
    rows_ref[8:16] = sum(stats_ref[p, 16:24] * shares[p] for p in parts) / total
    acc_ref[...] = jnp.zeros_like(acc_ref)

    def one_step(step):
        slot, spans, keys, query, grad, probs, score_grad = step_gradients(
            table_ref, kv_ref, q_ref, g_ref, rows_ref, step
        )
        dk = dot(score_grad, query, NN)
        dv = dot(probs.astype(jnp.bfloat16), grad, NN)
        for n in range(GROUP):
            acc_ref[spans[n]] += dk[n * SPAN : (n + 1) * SPAN]
            acc_ref[spans[n] + 2] += dv[n * SPAN : (n + 1) * SPAN]

    run_steps(table_ref, one_step)
    for n in range(2 * KEYS):
        scaling = SCALING if n % 4 < 2 else 1.0
        dkv_ref[n] = (acc_ref[n] * scaling).astype(jnp.bfloat16)


def query_kernel(
    place_ref,
    table_ref,
    kv_ref,
    q_ref,
    g_ref,
    rows_ref,
    after_ref,
    keep_ref,
    send_ref,
    acc_ref,
    log_ref,
    delta_ref,
):
    acc_ref[...] = jnp.zeros_like(acc_ref)
    for slot in range(SLOTS):
        log_ref[slot] = jnp.broadcast_to(rows_ref[slot : slot + 1], (HEAD, ROWS)).T
        delta_ref[slot] = jnp.broadcast_to(rows_ref[8 + slot : 9 + slot], (HEAD, ROWS)).T

    def one_step(step):
        slot, base = table_ref[SLOT + step], table_ref[BASE + step]
        spans, keys, values = load_keys(table_ref, kv_ref, step)
        query_pos = base + lax.broadcasted_iota(jnp.int32, (SPAN, HEAD), 0)
        first = start_of([table_ref[1 + n] for n in range(3)], query_pos)
        lane = lax.broadcasted_iota(jnp.int32, (1, HEAD), 1)
        raw = dot(q_ref[slot], keys, NT)
        products = dot(g_ref[slot], values, NT)
        log_total, delta = log_ref[slot], delta_ref[slot]
        parts = []
        for n in range(GROUP // 2):
            low, high = (table_ref[PLACES + step * GROUP + 2 * n + i] for i in range(2))
            pos = jnp.where(lane < SPAN, low, high) + lane % SPAN
            visible = (pos <= query_pos) & (pos >= first)
            cols = slice(n * HEAD, (n + 1) * HEAD)
            scores = raw[:, cols].reshape(HEADS, SPAN, HEAD) * (SCALING * LOG2E)
            scores = jnp.where(visible[None], scores, NEG_FILL).reshape(ROWS, HEAD)
            probs = jnp.exp2(scores - log_total)
            parts.append((probs * (products[:, cols] - delta)).astype(jnp.bfloat16))
        acc_ref[slot] += dot(jnp.concatenate(parts, axis=1), keys, NN)

    run_steps(table_ref, one_step)
    xl, core = place_ref[1], place_ref[2]
    for rel in range(2):
        chip = xl if rel == 0 else 1 - xl
        for half in range(2):
            rows = slice(half * SPAN, (half + 1) * SPAN)
            mine = chip * 4 + core * 2 + half
            theirs = chip * 4 + (1 - core) * 2 + half
            for h in range(HEADS):
                cols, at = slice(h * HEAD, (h + 1) * HEAD), slice(h * SPAN, (h + 1) * SPAN)
                keep_ref[rel, rows, cols] = acc_ref[mine, at, :] * SCALING
                send_ref[rel, rows, cols] = (acc_ref[theirs, at, :] * SCALING).astype(jnp.bfloat16)


def swap(block, axis):
    return lax.ppermute(block, axis, [(0, 1), (1, 0)])


def call(kernel, name, out_shape, in_specs, out_specs, scratch=(), aliases={}):
    return pl.pallas_call(
        kernel,
        out_shape=out_shape,
        in_specs=in_specs,
        out_specs=out_specs,
        scratch_shapes=scratch,
        input_output_aliases=aliases,
        compiler_params=pltpu.CompilerParams(vmem_limit_bytes=40 * 1024 * 1024),
        name=name,
    )


SMEM = pl.BlockSpec(memory_space=pltpu.SMEM)
VMEM = pl.BlockSpec(memory_space=pltpu.VMEM)


KEYS_VALUES = (2 * KEYS, SPAN, HEAD)
LAID_OUT = jax.ShapeDtypeStruct((SLOTS, ROWS, HEAD), jnp.bfloat16)


def prepare(order, place, episodes, own):
    return call(
        prepare_kernel,
        "prepare",
        (jax.ShapeDtypeStruct((TABLE,), jnp.int32), LAID_OUT, LAID_OUT),
        [SMEM, SMEM, VMEM, VMEM],
        (SMEM, VMEM, VMEM),
    )(order, place, episodes, own)


def row_stats(place, table, kv_all, other, q, g):
    return call(
        stats_kernel,
        "row_stats",
        (LAID_OUT, LAID_OUT, jax.ShapeDtypeStruct((24, ROWS), jnp.float32)),
        [SMEM, SMEM, VMEM, VMEM, VMEM, VMEM],
        (VMEM, VMEM, VMEM),
        [pltpu.VMEM((CHUNKS, SLOTS, ROWS), jnp.float32)] * 3,
        {4: 0, 5: 1},
    )(place, table, kv_all, other, q, g)


def key_value_gradients(table, kv_all, q, g, stats_all):
    return call(
        key_value_kernel,
        "key_value_gradients",
        (
            jax.ShapeDtypeStruct(KEYS_VALUES, jnp.bfloat16),
            jax.ShapeDtypeStruct((16, ROWS), jnp.float32),
        ),
        [SMEM, VMEM, VMEM, VMEM, VMEM],
        (VMEM, VMEM),
        [pltpu.VMEM(KEYS_VALUES, jnp.float32)],
    )(table, kv_all, q, g, stats_all)


def query_gradients(place, table, kv_all, q, g, rows, after):
    shape = (2, 2 * SPAN, HEADS * HEAD)
    return call(
        query_kernel,
        "query_gradients",
        (
            jax.ShapeDtypeStruct(shape, jnp.float32),
            jax.ShapeDtypeStruct(shape, jnp.bfloat16),
        ),
        [SMEM, SMEM, VMEM, VMEM, VMEM, VMEM, pl.BlockSpec(memory_space=pl.ANY)],
        (VMEM, VMEM),
        [pltpu.VMEM((SLOTS, ROWS, HEAD), jnp.float32)] * 3,
    )(place, table, kv_all, q, g, rows, after)


def per_device(query_rows, key_rows, stored_value_rows, output_grad, span_order, episode_ids):
    tokens = query_rows.shape[1]
    ring = lax.axis_size("y")
    place = jnp.stack([lax.axis_index("y"), lax.axis_index("xl"), lax.axis_index("core")]).astype(
        jnp.int32
    )
    part = lax.broadcasted_iota(jnp.int32, (ring, 2, tokens, HEAD), 1)
    kv = jnp.where(part == 0, key_rows[None], stored_value_rows[None])
    kv_all = lax.all_to_all(kv, "y", 0, 0, tiled=True).reshape(KEYS_VALUES)
    both = jnp.concatenate([query_rows[0], output_grad[0]], axis=1)
    remote = swap(both, "xl")
    own = lax.all_gather(both, "core", axis=0, tiled=True)
    other = lax.all_gather(remote, "core", axis=0, tiled=True)
    table, q, g = prepare(span_order, place, episode_ids, own)
    q, g, stats = row_stats(place, table, kv_all, other, q, g)
    stats_all = lax.all_gather(stats, ("xl", "core"), axis=0)
    dkv, rows = key_value_gradients(table, kv_all, q, g, stats_all)
    dkv_parts = lax.all_to_all(dkv.reshape(ring, 2 * tokens, HEAD), "y", 0, 0, tiled=True)
    keep, send = query_gradients(place, table, kv_all, q, g, rows, dkv)
    sent = lax.all_gather(send, "core", axis=0)
    dq = keep + lax.dynamic_index_in_dim(sent, 1 - place[2], 0, False).astype(jnp.float32)
    parts = dq.astype(jnp.bfloat16)
    straight = swap(parts[0], "section")
    across = lax.ppermute(parts[1], ("section", "xl"), [(0, 3), (1, 2), (2, 1), (3, 0)])
    dq_back = (straight.astype(jnp.float32) + across.astype(jnp.float32)).astype(jnp.bfloat16)
    dkv_sum = jnp.sum(dkv_parts.astype(jnp.float32), axis=0).astype(jnp.bfloat16)
    dkv_back = swap(dkv_sum, "section")
    return (dq_back[None], dkv_back[None, :tokens], dkv_back[None, tokens:])


def solution(mesh):
    devices = mesh.devices
    fine = Mesh(
        devices.reshape(devices.shape[0], devices.shape[1], devices.shape[2] // 4, 2, 2),
        ("section", "tp", "y", "xl", "core"),
    )
    rows = P("section", ("y", "xl", "core"), "tp")
    return jax.shard_map(
        per_device,
        mesh=fine,
        in_specs=(rows, rows, rows, rows, P(), P("section", None)),
        out_specs=(rows, rows, rows),
        check_vma=False,
    )
```

```python
import functools

import jax
import jax.numpy as jnp
from jax import lax
from jax.experimental import pallas as pl
from jax.experimental.pallas import tpu as pltpu
from jax.sharding import Mesh
from jax.sharding import PartitionSpec as P

HEAD = 128
SPAN = 64
HEADS = 6
ROWS = HEADS * SPAN
SLOTS = 8
KEYS = 16
GROUP = 4
UNROLLS = (8, 4, 2, 1)
CHUNKS = KEYS // GROUP
STEPS = SLOTS * CHUNKS + CHUNKS
SCALING = HEAD ** (-0.5)
LOG2E = 1.4426950408889634
NEG_FILL = -1e30
FAR = 1 << 20
NT = (((1,), (1,)), ((), ()))
NN = (((1,), (0,)), ((), ()))

SLOT = 16
CHUNK = SLOT + STEPS
BASE = CHUNK + STEPS
SPANS = BASE + STEPS
PLACES = SPANS + STEPS * GROUP
TABLE = PLACES + STEPS * GROUP


def dot(a, b, dims):
    return lax.dot_general(a, b, dims, preferred_element_type=jnp.float32)


def start_of(starts, pos):
    first = jnp.zeros_like(pos)
    for s in starts:
        first = jnp.maximum(first, jnp.where(s <= pos, s, 0))
    return first


def prepare_kernel(
    order_ref, place_ref, episode_ref, own_ref, table_ref, q_ref, g_ref
):
    y, xl, core = place_ref[0], place_ref[1], place_ref[2]
    ids = episode_ref[...]
    starts = [jnp.sum((ids < v).astype(jnp.int32)) for v in (1, 2, 3)]
    for n, s in enumerate(starts):
        table_ref[1 + n] = s
    key_bases = [
        order_ref[((k // 2) * 4 + xl * 2 + core) * 2 + k % 2] * SPAN for k in range(KEYS)
    ]

    def list_slot(slot, step):
        base = order_ref[y * SLOTS + slot] * SPAN
        first = start_of(starts, base)
        at = step * GROUP
        for k in range(KEYS):
            table_ref[SPANS + at] = (k // 2) * 4 + k % 2
            table_ref[PLACES + at] = key_bases[k]
            seen = (key_bases[k] <= base) & (key_bases[k] + (SPAN - 1) >= first)
            at = at + seen.astype(jnp.int32)
        count = (at - step * GROUP + GROUP - 1) // GROUP
        for extra in range(GROUP):
            table_ref[SPANS + at + extra] = 0
            table_ref[PLACES + at + extra] = FAR
        for c in range(CHUNKS):
            table_ref[SLOT + step + c] = slot
            table_ref[CHUNK + step + c] = c
            table_ref[BASE + step + c] = base
        return step + count

    table_ref[0] = lax.fori_loop(0, SLOTS, list_slot, jnp.int32(0))
    lay_out(own_ref, q_ref, g_ref, xl)


def lay_out(ref, q_ref, g_ref, chip):
    for n, out_ref in enumerate((q_ref, g_ref)):
        for i in range(SLOTS // 2):
            for h in range(HEADS):
                out_ref[chip * 4 + i, h * SPAN : (h + 1) * SPAN, :] = ref[
                    i * SPAN : (i + 1) * SPAN, (n * HEADS + h) * HEAD : (n * HEADS + h + 1) * HEAD
                ]


def load_keys(table_ref, kv_ref, step):
    spans = [table_ref[SPANS + step * GROUP + i] for i in range(GROUP)]
    keys = jnp.concatenate([kv_ref[s] for s in spans], axis=0)
    values = jnp.concatenate([kv_ref[s + 2] for s in spans], axis=0)
    return spans, keys, values


def load_step(table_ref, kv_ref, q_ref, g_ref, step):
    slot, base = table_ref[SLOT + step], table_ref[BASE + step]
    spans, keys, values = load_keys(table_ref, kv_ref, step)
    iota = lax.broadcasted_iota(jnp.int32, (SPAN, HEAD), 0)
    pos = jnp.concatenate(
        [table_ref[PLACES + step * GROUP + i] + iota for i in range(GROUP)], axis=0
    )
    query_pos = base + lax.broadcasted_iota(jnp.int32, (1, HEAD), 1) % SPAN
    first = start_of([table_ref[1 + n] for n in range(3)], query_pos)
    visible = (pos <= query_pos) & (pos >= first)
    query, grad = q_ref[slot], g_ref[slot]
    raw = dot(keys, query, NT)
    scores = jnp.concatenate(
        [
            jnp.where(visible, raw[:, g * HEAD : (g + 1) * HEAD] * (SCALING * LOG2E), NEG_FILL)
            for g in range(ROWS // HEAD)
        ],
        axis=1,
    )
    return slot, spans, keys, query, grad, scores, dot(values, grad, NT)


def run_steps(table_ref, one_step):
    at, count = jnp.int32(0), table_ref[0]
    for steps in UNROLLS:

        def some(n, unused, at=at, steps=steps):
            for i in range(steps):
                one_step(at + n * steps + i)
            return unused

        turns = (count - at) // steps
        lax.fori_loop(0, turns, some, 0)
        at = at + turns * steps


def stats_kernel(
    place_ref,
    table_ref,
    kv_ref,
    other_ref,
    q_in_ref,
    g_in_ref,
    q_ref,
    g_ref,
    out_ref,
    top_ref,
    total_ref,
    weighted_ref,
):
    lay_out(other_ref, q_ref, g_ref, 1 - place_ref[1])
    top_ref[...] = jnp.full_like(top_ref, NEG_FILL)
    total_ref[...] = jnp.zeros_like(total_ref)
    weighted_ref[...] = jnp.zeros_like(weighted_ref)

    def one_step(step):
        slot, spans, keys, query, grad, scores, products = load_step(
            table_ref, kv_ref, q_ref, g_ref, step
        )
        chunk = table_ref[CHUNK + step]
        top = jnp.max(scores, axis=0, keepdims=True)
        weights = jnp.exp2(scores - top)
        row = pl.ds(slot, 1)
        top_ref[chunk, row, :] = top
        total_ref[chunk, row, :] = jnp.sum(weights, axis=0, keepdims=True)
        weighted_ref[chunk, row, :] = jnp.sum(weights * products, axis=0, keepdims=True)

    run_steps(table_ref, one_step)
    parts = range(CHUNKS)
    top = functools.reduce(jnp.maximum, [top_ref[c] for c in parts])
    shares = [jnp.exp2(top_ref[c] - top) for c in parts]
    out_ref[0:8] = top
    out_ref[8:16] = sum(total_ref[c] * shares[c] for c in parts)
    out_ref[16:24] = sum(weighted_ref[c] * shares[c] for c in parts)


def step_gradients(table_ref, kv_ref, q_ref, g_ref, rows_ref, step):
    slot, spans, keys, query, grad, scores, products = load_step(
        table_ref, kv_ref, q_ref, g_ref, step
    )
    probs = jnp.exp2(scores - rows_ref[pl.ds(slot, 1), :])
    score_grad = (probs * (products - rows_ref[pl.ds(8 + slot, 1), :])).astype(jnp.bfloat16)
    return slot, spans, keys, query, grad, probs, score_grad


def key_value_kernel(table_ref, kv_ref, q_ref, g_ref, stats_ref, dkv_ref, rows_ref, acc_ref):
    parts = range(stats_ref.shape[0])
    top = functools.reduce(jnp.maximum, [stats_ref[p, 0:8] for p in parts])
    shares = [jnp.exp2(stats_ref[p, 0:8] - top) for p in parts]
    total = sum(stats_ref[p, 8:16] * shares[p] for p in parts)
    rows_ref[0:8] = top + jnp.log2(total)
    rows_ref[8:16] = sum(stats_ref[p, 16:24] * shares[p] for p in parts) / total
    acc_ref[...] = jnp.zeros_like(acc_ref)

    def one_step(step):
        slot, spans, keys, query, grad, probs, score_grad = step_gradients(
            table_ref, kv_ref, q_ref, g_ref, rows_ref, step
        )
        dk = dot(score_grad, query, NN)
        dv = dot(probs.astype(jnp.bfloat16), grad, NN)
        for n in range(GROUP):
            acc_ref[spans[n]] += dk[n * SPAN : (n + 1) * SPAN]
            acc_ref[spans[n] + 2] += dv[n * SPAN : (n + 1) * SPAN]

    run_steps(table_ref, one_step)
    for n in range(2 * KEYS):
        scaling = SCALING if n % 4 < 2 else 1.0
        dkv_ref[n] = (acc_ref[n] * scaling).astype(jnp.bfloat16)


def query_kernel(
    place_ref,
    table_ref,
    kv_ref,
    q_ref,
    g_ref,
    rows_ref,
    after_ref,
    keep_ref,
    send_ref,
    acc_ref,
    log_ref,
    delta_ref,
):
    acc_ref[...] = jnp.zeros_like(acc_ref)
    for slot in range(SLOTS):
        log_ref[slot] = jnp.broadcast_to(rows_ref[slot : slot + 1], (HEAD, ROWS)).T
        delta_ref[slot] = jnp.broadcast_to(rows_ref[8 + slot : 9 + slot], (HEAD, ROWS)).T

    def one_step(step):
        slot, base = table_ref[SLOT + step], table_ref[BASE + step]
        spans, keys, values = load_keys(table_ref, kv_ref, step)
        query_pos = base + lax.broadcasted_iota(jnp.int32, (SPAN, HEAD), 0)
        first = start_of([table_ref[1 + n] for n in range(3)], query_pos)
        lane = lax.broadcasted_iota(jnp.int32, (1, HEAD), 1)
        raw = dot(q_ref[slot], keys, NT)
        products = dot(g_ref[slot], values, NT)
        log_total, delta = log_ref[slot], delta_ref[slot]
        parts = []
        for n in range(GROUP // 2):
            low, high = (table_ref[PLACES + step * GROUP + 2 * n + i] for i in range(2))
            pos = jnp.where(lane < SPAN, low, high) + lane % SPAN
            visible = (pos <= query_pos) & (pos >= first)
            cols = slice(n * HEAD, (n + 1) * HEAD)
            scores = raw[:, cols].reshape(HEADS, SPAN, HEAD) * (SCALING * LOG2E)
            scores = jnp.where(visible[None], scores, NEG_FILL).reshape(ROWS, HEAD)
            probs = jnp.exp2(scores - log_total)
            parts.append((probs * (products[:, cols] - delta)).astype(jnp.bfloat16))
        acc_ref[slot] += dot(jnp.concatenate(parts, axis=1), keys, NN)

    run_steps(table_ref, one_step)
    xl, core = place_ref[1], place_ref[2]
    for rel in range(2):
        chip = xl if rel == 0 else 1 - xl
        for half in range(2):
            rows = slice(half * SPAN, (half + 1) * SPAN)
            mine = chip * 4 + core * 2 + half
            theirs = chip * 4 + (1 - core) * 2 + half
            for h in range(HEADS):
                cols, at = slice(h * HEAD, (h + 1) * HEAD), slice(h * SPAN, (h + 1) * SPAN)
                keep_ref[rel, rows, cols] = acc_ref[mine, at, :] * SCALING
                send_ref[rel, rows, cols] = (acc_ref[theirs, at, :] * SCALING).astype(jnp.bfloat16)


def swap(block, axis):
    return lax.ppermute(block, axis, [(0, 1), (1, 0)])


def call(kernel, name, out_shape, in_specs, out_specs, scratch=(), aliases={}):
    return pl.pallas_call(
        kernel,
        out_shape=out_shape,
        in_specs=in_specs,
        out_specs=out_specs,
        scratch_shapes=scratch,
        input_output_aliases=aliases,
        compiler_params=pltpu.CompilerParams(vmem_limit_bytes=40 * 1024 * 1024),
        name=name,
    )


SMEM = pl.BlockSpec(memory_space=pltpu.SMEM)
VMEM = pl.BlockSpec(memory_space=pltpu.VMEM)


KEYS_VALUES = (2 * KEYS, SPAN, HEAD)
LAID_OUT = jax.ShapeDtypeStruct((SLOTS, ROWS, HEAD), jnp.bfloat16)


def prepare(order, place, episodes, own):
    return call(
        prepare_kernel,
        "prepare",
        (jax.ShapeDtypeStruct((TABLE,), jnp.int32), LAID_OUT, LAID_OUT),
        [SMEM, SMEM, VMEM, VMEM],
        (SMEM, VMEM, VMEM),
    )(order, place, episodes, own)


def row_stats(place, table, kv_all, other, q, g):
    return call(
        stats_kernel,
        "row_stats",
        (LAID_OUT, LAID_OUT, jax.ShapeDtypeStruct((24, ROWS), jnp.float32)),
        [SMEM, SMEM, VMEM, VMEM, VMEM, VMEM],
        (VMEM, VMEM, VMEM),
        [pltpu.VMEM((CHUNKS, SLOTS, ROWS), jnp.float32)] * 3,
        {4: 0, 5: 1},
    )(place, table, kv_all, other, q, g)


def key_value_gradients(table, kv_all, q, g, stats_all):
    return call(
        key_value_kernel,
        "key_value_gradients",
        (
            jax.ShapeDtypeStruct(KEYS_VALUES, jnp.bfloat16),
            jax.ShapeDtypeStruct((16, ROWS), jnp.float32),
        ),
        [SMEM, VMEM, VMEM, VMEM, VMEM],
        (VMEM, VMEM),
        [pltpu.VMEM(KEYS_VALUES, jnp.float32)],
    )(table, kv_all, q, g, stats_all)


def query_gradients(place, table, kv_all, q, g, rows, after):
    shape = (2, 2 * SPAN, HEADS * HEAD)
    return call(
        query_kernel,
        "query_gradients",
        (
            jax.ShapeDtypeStruct(shape, jnp.float32),
            jax.ShapeDtypeStruct(shape, jnp.bfloat16),
        ),
        [SMEM, SMEM, VMEM, VMEM, VMEM, VMEM, pl.BlockSpec(memory_space=pl.ANY)],
        (VMEM, VMEM),
        [pltpu.VMEM((SLOTS, ROWS, HEAD), jnp.float32)] * 3,
    )(place, table, kv_all, q, g, rows, after)


def per_device(query_rows, key_rows, stored_value_rows, output_grad, span_order, episode_ids):
    tokens = query_rows.shape[1]
    ring = lax.axis_size("y")
    place = jnp.stack([lax.axis_index("y"), lax.axis_index("xl"), lax.axis_index("core")]).astype(
        jnp.int32
    )
    part = lax.broadcasted_iota(jnp.int32, (ring, 2, tokens, HEAD), 1)
    kv = jnp.where(part == 0, key_rows[None], stored_value_rows[None])
    kv_all = lax.all_to_all(kv, "y", 0, 0, tiled=True).reshape(KEYS_VALUES)
    both = jnp.concatenate([query_rows[0], output_grad[0]], axis=1)
    remote = swap(both, "xl")
    own = lax.all_gather(both, "core", axis=0, tiled=True)
    other = lax.all_gather(remote, "core", axis=0, tiled=True)
    table, q, g = prepare(span_order, place, episode_ids, own)
    q, g, stats = row_stats(place, table, kv_all, other, q, g)
    stats_all = lax.all_gather(stats, ("xl", "core"), axis=0)
    dkv, rows = key_value_gradients(table, kv_all, q, g, stats_all)
    dkv_parts = lax.all_to_all(dkv.reshape(ring, 2 * tokens, HEAD), "y", 0, 0, tiled=True)
    keep, send = query_gradients(place, table, kv_all, q, g, rows, dkv)
    sent = lax.all_gather(send, "core", axis=0)
    dq = keep + lax.dynamic_index_in_dim(sent, 1 - place[2], 0, False).astype(jnp.float32)
    parts = dq.astype(jnp.bfloat16)
    across = lax.ppermute(parts[1], ("section", "xl"), [(0, 3), (1, 2), (2, 1), (3, 0)])
    straight = swap(parts[0], "section")
    dkv_sum = jnp.sum(dkv_parts.astype(jnp.float32), axis=0).astype(jnp.bfloat16)
    both_dkv = lax.all_gather(dkv_sum, "section", axis=0)
    dkv_back = lax.dynamic_slice_in_dim(both_dkv, 1 - lax.axis_index("section"), 1, 0)
    dk_back, dv_back = dkv_back[:, :tokens], dkv_back[:, tokens:]
    straight, across, dk_back, dv_back = lax.optimization_barrier(
        (straight, across, dk_back, dv_back)
    )
    dq_back = (straight.astype(jnp.float32) + across.astype(jnp.float32)).astype(jnp.bfloat16)
    return (dq_back[None], dk_back, dv_back)


def solution(mesh):
    devices = mesh.devices
    fine = Mesh(
        devices.reshape(devices.shape[0], devices.shape[1], devices.shape[2] // 4, 2, 2),
        ("section", "tp", "y", "xl", "core"),
    )
    rows = P("section", ("y", "xl", "core"), "tp")
    return jax.shard_map(
        per_device,
        mesh=fine,
        in_specs=(rows, rows, rows, rows, P(), P("section", None)),
        out_specs=(rows, rows, rows),
        check_vma=False,
    )
```

```python
import functools

import jax
import jax.numpy as jnp
from jax import lax
from jax.experimental import pallas as pl
from jax.experimental.pallas import tpu as pltpu
from jax.sharding import Mesh
from jax.sharding import PartitionSpec as P

HEAD = 128
SPAN = 64
HEADS = 6
ROWS = HEADS * SPAN
SLOTS = 8
KEYS = 16
GROUP = 4
UNROLLS = (8, 4, 2, 1)
CHUNKS = KEYS // GROUP
STEPS = SLOTS * CHUNKS + 2 * CHUNKS
SCALING = HEAD ** (-0.5)
LOG2E = 1.4426950408889634
NEG_FILL = -1e30
FAR = 1 << 20
NT = (((1,), (1,)), ((), ()))
NN = (((1,), (0,)), ((), ()))

SLOT = 16
CHUNK = SLOT + STEPS
BASE = CHUNK + STEPS
SPANS = BASE + STEPS
PLACES = SPANS + STEPS * GROUP
TABLE = PLACES + STEPS * GROUP


def dot(a, b, dims):
    return lax.dot_general(a, b, dims, preferred_element_type=jnp.float32)


def start_of(starts, pos):
    first = jnp.zeros_like(pos)
    for s in starts:
        first = jnp.maximum(first, jnp.where(s <= pos, s, 0))
    return first


def list_span(table_ref, starts, step, slot, base, keys, chunk):
    first = start_of(starts, base)
    at = step * GROUP
    for number, place in keys:
        table_ref[SPANS + at] = number
        table_ref[PLACES + at] = place
        seen = (place <= base) & (place + (SPAN - 1) >= first)
        at = at + seen.astype(jnp.int32)
    count = (at - step * GROUP + GROUP - 1) // GROUP
    for extra in range(GROUP):
        table_ref[SPANS + at + extra] = 0
        table_ref[PLACES + at + extra] = FAR
    for c in range(len(keys) // GROUP):
        table_ref[SLOT + step + c] = slot
        table_ref[CHUNK + step + c] = c if chunk is None else chunk
        table_ref[BASE + step + c] = base
    return step + count


def prepare_kernel(
    order_ref, place_ref, episode_ref, own_ref, table_ref, query_table_ref, q_ref, g_ref
):
    y, xl, core = place_ref[0], place_ref[1], place_ref[2]
    ids = episode_ref[...]
    starts = [jnp.sum((ids < v).astype(jnp.int32)) for v in (1, 2, 3)]
    for n, s in enumerate(starts):
        table_ref[1 + n] = s
        query_table_ref[1 + n] = s

    def keys_of(side):
        return [
            ((k // 2) * 4 + k % 2, order_ref[((k // 2) * 4 + xl * 2 + side) * 2 + k % 2] * SPAN)
            for k in range(KEYS)
        ]

    keys = keys_of(core)

    def list_slot(slot, step):
        base = order_ref[y * SLOTS + slot] * SPAN
        return list_span(table_ref, starts, step, slot, base, keys, None)

    table_ref[0] = lax.fori_loop(0, SLOTS, list_slot, jnp.int32(0))
    both = keys + [(2 * KEYS + number, place) for number, place in keys_of(1 - core)]

    def list_own_slot(n, step):
        slot = n // 2 * 4 + core * 2 + n % 2
        base = order_ref[y * SLOTS + slot] * SPAN
        return list_span(query_table_ref, starts, step, slot, base, both, n)

    query_table_ref[0] = lax.fori_loop(0, SLOTS // 2, list_own_slot, jnp.int32(0))
    lay_out(own_ref, q_ref, g_ref, xl)


def lay_out(ref, q_ref, g_ref, chip):
    for n, out_ref in enumerate((q_ref, g_ref)):
        for i in range(SLOTS // 2):
            for h in range(HEADS):
                out_ref[chip * 4 + i, h * SPAN : (h + 1) * SPAN, :] = ref[
                    i * SPAN : (i + 1) * SPAN, (n * HEADS + h) * HEAD : (n * HEADS + h + 1) * HEAD
                ]


def load_keys(table_ref, kv_ref, step):
    spans = [table_ref[SPANS + step * GROUP + i] for i in range(GROUP)]
    keys = jnp.concatenate([kv_ref[s] for s in spans], axis=0)
    values = jnp.concatenate([kv_ref[s + 2] for s in spans], axis=0)
    return spans, keys, values


def load_step(table_ref, kv_ref, q_ref, g_ref, step):
    slot, base = table_ref[SLOT + step], table_ref[BASE + step]
    spans, keys, values = load_keys(table_ref, kv_ref, step)
    iota = lax.broadcasted_iota(jnp.int32, (SPAN, HEAD), 0)
    pos = jnp.concatenate(
        [table_ref[PLACES + step * GROUP + i] + iota for i in range(GROUP)], axis=0
    )
    query_pos = base + lax.broadcasted_iota(jnp.int32, (1, HEAD), 1) % SPAN
    first = start_of([table_ref[1 + n] for n in range(3)], query_pos)
    visible = (pos <= query_pos) & (pos >= first)
    query, grad = q_ref[slot], g_ref[slot]
    raw = dot(keys, query, NT)
    scores = jnp.concatenate(
        [
            jnp.where(visible, raw[:, g * HEAD : (g + 1) * HEAD] * (SCALING * LOG2E), NEG_FILL)
            for g in range(ROWS // HEAD)
        ],
        axis=1,
    )
    return slot, spans, keys, query, grad, scores, dot(values, grad, NT)


def run_steps(table_ref, one_step):
    at, count = jnp.int32(0), table_ref[0]
    for steps in UNROLLS:

        def some(n, unused, at=at, steps=steps):
            for i in range(steps):
                one_step(at + n * steps + i)
            return unused

        turns = (count - at) // steps
        lax.fori_loop(0, turns, some, 0)
        at = at + turns * steps


def stats_kernel(
    place_ref,
    table_ref,
    kv_ref,
    other_ref,
    q_in_ref,
    g_in_ref,
    q_ref,
    g_ref,
    out_ref,
    top_ref,
    total_ref,
    weighted_ref,
):
    lay_out(other_ref, q_ref, g_ref, 1 - place_ref[1])
    top_ref[...] = jnp.full_like(top_ref, NEG_FILL)
    total_ref[...] = jnp.zeros_like(total_ref)
    weighted_ref[...] = jnp.zeros_like(weighted_ref)

    def one_step(step):
        slot, spans, keys, query, grad, scores, products = load_step(
            table_ref, kv_ref, q_ref, g_ref, step
        )
        chunk = table_ref[CHUNK + step]
        top = jnp.max(scores, axis=0, keepdims=True)
        weights = jnp.exp2(scores - top)
        row = pl.ds(slot, 1)
        top_ref[chunk, row, :] = top
        total_ref[chunk, row, :] = jnp.sum(weights, axis=0, keepdims=True)
        weighted_ref[chunk, row, :] = jnp.sum(weights * products, axis=0, keepdims=True)

    run_steps(table_ref, one_step)
    parts = range(CHUNKS)
    top = functools.reduce(jnp.maximum, [top_ref[c] for c in parts])
    shares = [jnp.exp2(top_ref[c] - top) for c in parts]
    out_ref[0:8] = top
    out_ref[8:16] = sum(total_ref[c] * shares[c] for c in parts)
    out_ref[16:24] = sum(weighted_ref[c] * shares[c] for c in parts)


def step_gradients(table_ref, kv_ref, q_ref, g_ref, rows_ref, step):
    slot, spans, keys, query, grad, scores, products = load_step(
        table_ref, kv_ref, q_ref, g_ref, step
    )
    probs = jnp.exp2(scores - rows_ref[pl.ds(slot, 1), :])
    score_grad = (probs * (products - rows_ref[pl.ds(8 + slot, 1), :])).astype(jnp.bfloat16)
    return slot, spans, keys, query, grad, probs, score_grad


def key_value_kernel(table_ref, kv_ref, q_ref, g_ref, stats_ref, dkv_ref, rows_ref, acc_ref):
    parts = range(stats_ref.shape[0])
    top = functools.reduce(jnp.maximum, [stats_ref[p, 0:8] for p in parts])
    shares = [jnp.exp2(stats_ref[p, 0:8] - top) for p in parts]
    total = sum(stats_ref[p, 8:16] * shares[p] for p in parts)
    rows_ref[0:8] = top + jnp.log2(total)
    rows_ref[8:16] = sum(stats_ref[p, 16:24] * shares[p] for p in parts) / total
    acc_ref[...] = jnp.zeros_like(acc_ref)

    def one_step(step):
        slot, spans, keys, query, grad, probs, score_grad = step_gradients(
            table_ref, kv_ref, q_ref, g_ref, rows_ref, step
        )
        dk = dot(score_grad, query, NN)
        dv = dot(probs.astype(jnp.bfloat16), grad, NN)
        for n in range(GROUP):
            acc_ref[spans[n]] += dk[n * SPAN : (n + 1) * SPAN]
            acc_ref[spans[n] + 2] += dv[n * SPAN : (n + 1) * SPAN]

    run_steps(table_ref, one_step)
    for n in range(2 * KEYS):
        scaling = SCALING if n % 4 < 2 else 1.0
        dkv_ref[n] = (acc_ref[n] * scaling).astype(jnp.bfloat16)


def query_kernel(
    place_ref,
    table_ref,
    own_ref,
    far_ref,
    q_ref,
    g_ref,
    rows_ref,
    out_ref,
    acc_ref,
    log_ref,
    delta_ref,
    kv_ref,
):
    xl, core = place_ref[1], place_ref[2]
    kv_ref[: 2 * KEYS] = own_ref[...]
    kv_ref[2 * KEYS :] = far_ref[...]
    acc_ref[...] = jnp.zeros_like(acc_ref)
    for n in range(SLOTS // 2):
        slot = n // 2 * 4 + core * 2 + n % 2
        log_ref[n] = jnp.broadcast_to(rows_ref[pl.ds(slot, 1), :], (HEAD, ROWS)).T
        delta_ref[n] = jnp.broadcast_to(rows_ref[pl.ds(8 + slot, 1), :], (HEAD, ROWS)).T

    def one_step(step):
        slot, own = table_ref[SLOT + step], table_ref[CHUNK + step]
        base = table_ref[BASE + step]
        spans, keys, values = load_keys(table_ref, kv_ref, step)
        query_pos = base + lax.broadcasted_iota(jnp.int32, (SPAN, HEAD), 0)
        first = start_of([table_ref[1 + n] for n in range(3)], query_pos)
        lane = lax.broadcasted_iota(jnp.int32, (1, HEAD), 1)
        raw = dot(q_ref[slot], keys, NT)
        products = dot(g_ref[slot], values, NT)
        log_total, delta = log_ref[own], delta_ref[own]
        parts = []
        for n in range(GROUP // 2):
            low, high = (table_ref[PLACES + step * GROUP + 2 * n + i] for i in range(2))
            pos = jnp.where(lane < SPAN, low, high) + lane % SPAN
            visible = (pos <= query_pos) & (pos >= first)
            cols = slice(n * HEAD, (n + 1) * HEAD)
            scores = raw[:, cols].reshape(HEADS, SPAN, HEAD) * (SCALING * LOG2E)
            scores = jnp.where(visible[None], scores, NEG_FILL).reshape(ROWS, HEAD)
            probs = jnp.exp2(scores - log_total)
            parts.append((probs * (products[:, cols] - delta)).astype(jnp.bfloat16))
        acc_ref[own] += dot(jnp.concatenate(parts, axis=1), keys, NN)

    run_steps(table_ref, one_step)
    for rel in range(2):
        chip = xl if rel == 0 else 1 - xl
        for half in range(2):
            for h in range(HEADS):
                block = acc_ref[chip * 2 + half, h * SPAN : (h + 1) * SPAN, :] * SCALING
                rows, cols = slice(half * SPAN, (half + 1) * SPAN), slice(h * HEAD, (h + 1) * HEAD)
                out_ref[rel, rows, cols] = block.astype(jnp.bfloat16)


def swap(block, axis):
    return lax.ppermute(block, axis, [(0, 1), (1, 0)])


def call(kernel, name, out_shape, in_specs, out_specs, scratch=(), aliases={}):
    return pl.pallas_call(
        kernel,
        out_shape=out_shape,
        in_specs=in_specs,
        out_specs=out_specs,
        scratch_shapes=scratch,
        input_output_aliases=aliases,
        compiler_params=pltpu.CompilerParams(vmem_limit_bytes=40 * 1024 * 1024),
        name=name,
    )


SMEM = pl.BlockSpec(memory_space=pltpu.SMEM)
VMEM = pl.BlockSpec(memory_space=pltpu.VMEM)


KEYS_VALUES = (2 * KEYS, SPAN, HEAD)
LAID_OUT = jax.ShapeDtypeStruct((SLOTS, ROWS, HEAD), jnp.bfloat16)


def prepare(order, place, episodes, own):
    return call(
        prepare_kernel,
        "prepare",
        (*[jax.ShapeDtypeStruct((TABLE,), jnp.int32)] * 2, LAID_OUT, LAID_OUT),
        [SMEM, SMEM, VMEM, VMEM],
        (SMEM, SMEM, VMEM, VMEM),
    )(order, place, episodes, own)


def row_stats(place, table, kv_all, other, q, g):
    return call(
        stats_kernel,
        "row_stats",
        (LAID_OUT, LAID_OUT, jax.ShapeDtypeStruct((24, ROWS), jnp.float32)),
        [SMEM, SMEM, VMEM, VMEM, VMEM, VMEM],
        (VMEM, VMEM, VMEM),
        [pltpu.VMEM((CHUNKS, SLOTS, ROWS), jnp.float32)] * 3,
        {4: 0, 5: 1},
    )(place, table, kv_all, other, q, g)


def key_value_gradients(table, kv_all, q, g, stats_all):
    return call(
        key_value_kernel,
        "key_value_gradients",
        (
            jax.ShapeDtypeStruct(KEYS_VALUES, jnp.bfloat16),
            jax.ShapeDtypeStruct((16, ROWS), jnp.float32),
        ),
        [SMEM, VMEM, VMEM, VMEM, VMEM],
        (VMEM, VMEM),
        [pltpu.VMEM(KEYS_VALUES, jnp.float32)],
    )(table, kv_all, q, g, stats_all)


def query_gradients(place, table, kv_own, kv_far, q, g, rows):
    return call(
        query_kernel,
        "query_gradients",
        jax.ShapeDtypeStruct((2, 2 * SPAN, HEADS * HEAD), jnp.bfloat16),
        [SMEM, SMEM, VMEM, VMEM, VMEM, VMEM, VMEM],
        VMEM,
        [pltpu.VMEM((SLOTS // 2, ROWS, HEAD), jnp.float32)] * 3
        + [pltpu.VMEM((4 * KEYS, SPAN, HEAD), jnp.bfloat16)],
    )(place, table, kv_own, kv_far, q, g, rows)


def per_device(query_rows, key_rows, stored_value_rows, output_grad, span_order, episode_ids):
    tokens = query_rows.shape[1]
    ring = lax.axis_size("y")
    place = jnp.stack([lax.axis_index("y"), lax.axis_index("xl"), lax.axis_index("core")]).astype(
        jnp.int32
    )
    part = lax.broadcasted_iota(jnp.int32, (ring, 2, tokens, HEAD), 1)
    kv = jnp.where(part == 0, key_rows[None], stored_value_rows[None])
    kv_all = lax.all_to_all(kv, "y", 0, 0, tiled=True).reshape(KEYS_VALUES)
    both = jnp.concatenate([query_rows[0], output_grad[0]], axis=1)
    remote = swap(both, "xl")
    own = lax.all_gather(both, "core", axis=0, tiled=True)
    other = lax.all_gather(remote, "core", axis=0, tiled=True)
    table, query_table, q, g = prepare(span_order, place, episode_ids, own)
    q, g, stats = row_stats(place, table, kv_all, other, q, g)
    stats_all = lax.all_gather(stats, ("xl", "core"), axis=0)
    dkv, rows = key_value_gradients(table, kv_all, q, g, stats_all)
    dkv_parts = lax.all_to_all(dkv.reshape(ring, 2 * tokens, HEAD), "y", 0, 0, tiled=True)
    kv_late, unused = lax.optimization_barrier((kv_all, dkv))
    kv_far = swap(kv_late, "core")
    parts = query_gradients(place, query_table, kv_all, kv_far, q, g, rows)
    across = lax.ppermute(parts[1], ("section", "xl"), [(0, 3), (1, 2), (2, 1), (3, 0)])
    straight = swap(parts[0], "section")
    dkv_sum = jnp.sum(dkv_parts.astype(jnp.float32), axis=0).astype(jnp.bfloat16)
    both_dkv = lax.all_gather(dkv_sum, "section", axis=0)
    dkv_back = lax.dynamic_slice_in_dim(both_dkv, 1 - lax.axis_index("section"), 1, 0)
    dk_back, dv_back = dkv_back[:, :tokens], dkv_back[:, tokens:]
    straight, across, dk_back, dv_back = lax.optimization_barrier(
        (straight, across, dk_back, dv_back)
    )
    dq_back = (straight.astype(jnp.float32) + across.astype(jnp.float32)).astype(jnp.bfloat16)
    return (dq_back[None], dk_back, dv_back)


def solution(mesh):
    devices = mesh.devices
    fine = Mesh(
        devices.reshape(devices.shape[0], devices.shape[1], devices.shape[2] // 4, 2, 2),
        ("section", "tp", "y", "xl", "core"),
    )
    rows = P("section", ("y", "xl", "core"), "tp")
    return jax.shard_map(
        per_device,
        mesh=fine,
        in_specs=(rows, rows, rows, rows, P(), P("section", None)),
        out_specs=(rows, rows, rows),
        check_vma=False,
    )
```

```python
import functools

import jax
import jax.numpy as jnp
from jax import lax
from jax.experimental import pallas as pl
from jax.experimental.pallas import tpu as pltpu
from jax.sharding import Mesh
from jax.sharding import PartitionSpec as P

HEAD = 128
SPAN = 64
HEADS = 6
ROWS = HEADS * SPAN
SLOTS = 8
KEYS = 16
GROUP = 4
UNROLLS = (8, 4, 2, 1)
CHUNKS = KEYS // GROUP
STEPS = SLOTS * CHUNKS + 2 * CHUNKS
SCALING = HEAD ** (-0.5)
LOG2E = 1.4426950408889634
NEG_FILL = -1e30
FAR = 1 << 20
NT = (((1,), (1,)), ((), ()))
NN = (((1,), (0,)), ((), ()))

SLOT = 16
CHUNK = SLOT + STEPS
BASE = CHUNK + STEPS
SPANS = BASE + STEPS
PLACES = SPANS + STEPS * GROUP
TABLE = PLACES + STEPS * GROUP


def dot(a, b, dims):
    return lax.dot_general(a, b, dims, preferred_element_type=jnp.float32)


def start_of(starts, pos):
    first = jnp.zeros_like(pos)
    for s in starts:
        first = jnp.maximum(first, jnp.where(s <= pos, s, 0))
    return first


def list_span(table_ref, starts, step, slot, base, keys, chunk):
    first = start_of(starts, base)
    at = step * GROUP
    for number, place in keys:
        table_ref[SPANS + at] = number
        table_ref[PLACES + at] = place
        seen = (place <= base) & (place + (SPAN - 1) >= first)
        at = at + seen.astype(jnp.int32)
    count = (at - step * GROUP + GROUP - 1) // GROUP
    for extra in range(GROUP):
        table_ref[SPANS + at + extra] = 0
        table_ref[PLACES + at + extra] = FAR
    for c in range(len(keys) // GROUP):
        table_ref[SLOT + step + c] = slot
        table_ref[CHUNK + step + c] = c if chunk is None else chunk
        table_ref[BASE + step + c] = base
    return step + count


def prepare_kernel(
    order_ref, place_ref, episode_ref, own_ref, table_ref, near_ref, far_ref, q_ref, g_ref
):
    y, xl, core = place_ref[0], place_ref[1], place_ref[2]
    ids = episode_ref[...]
    starts = [jnp.sum((ids < v).astype(jnp.int32)) for v in (1, 2, 3)]
    for n, s in enumerate(starts):
        for ref in (table_ref, near_ref, far_ref):
            ref[1 + n] = s

    def keys_of(side):
        return [
            ((k // 2) * 4 + k % 2, order_ref[((k // 2) * 4 + xl * 2 + side) * 2 + k % 2] * SPAN)
            for k in range(KEYS)
        ]

    keys = keys_of(core)

    def list_slot(slot, step):
        base = order_ref[y * SLOTS + slot] * SPAN
        return list_span(table_ref, starts, step, slot, base, keys, None)

    table_ref[0] = lax.fori_loop(0, SLOTS, list_slot, jnp.int32(0))
    for ref, some_keys in ((near_ref, keys), (far_ref, keys_of(1 - core))):

        def list_own_slot(n, step, ref=ref, some_keys=some_keys):
            slot = n // 2 * 4 + core * 2 + n % 2
            base = order_ref[y * SLOTS + slot] * SPAN
            return list_span(ref, starts, step, slot, base, some_keys, n)

        ref[0] = lax.fori_loop(0, SLOTS // 2, list_own_slot, jnp.int32(0))
    lay_out(own_ref, q_ref, g_ref, xl)


def lay_out(ref, q_ref, g_ref, chip):
    for n, out_ref in enumerate((q_ref, g_ref)):
        for i in range(SLOTS // 2):
            for h in range(HEADS):
                out_ref[chip * 4 + i, h * SPAN : (h + 1) * SPAN, :] = ref[
                    i * SPAN : (i + 1) * SPAN, (n * HEADS + h) * HEAD : (n * HEADS + h + 1) * HEAD
                ]


def load_keys(table_ref, kv_ref, step):
    spans = [table_ref[SPANS + step * GROUP + i] for i in range(GROUP)]
    keys = jnp.concatenate([kv_ref[s] for s in spans], axis=0)
    values = jnp.concatenate([kv_ref[s + 2] for s in spans], axis=0)
    return spans, keys, values


def load_step(table_ref, kv_ref, q_ref, g_ref, step):
    slot, base = table_ref[SLOT + step], table_ref[BASE + step]
    spans, keys, values = load_keys(table_ref, kv_ref, step)
    iota = lax.broadcasted_iota(jnp.int32, (SPAN, HEAD), 0)
    pos = jnp.concatenate(
        [table_ref[PLACES + step * GROUP + i] + iota for i in range(GROUP)], axis=0
    )
    query_pos = base + lax.broadcasted_iota(jnp.int32, (1, HEAD), 1) % SPAN
    first = start_of([table_ref[1 + n] for n in range(3)], query_pos)
    visible = (pos <= query_pos) & (pos >= first)
    query, grad = q_ref[slot], g_ref[slot]
    raw = dot(keys, query, NT)
    scores = jnp.concatenate(
        [
            jnp.where(visible, raw[:, g * HEAD : (g + 1) * HEAD] * (SCALING * LOG2E), NEG_FILL)
            for g in range(ROWS // HEAD)
        ],
        axis=1,
    )
    return slot, spans, keys, query, grad, scores, dot(values, grad, NT)


def run_steps(table_ref, one_step):
    at, count = jnp.int32(0), table_ref[0]
    for steps in UNROLLS:

        def some(n, unused, at=at, steps=steps):
            for i in range(steps):
                one_step(at + n * steps + i)
            return unused

        turns = (count - at) // steps
        lax.fori_loop(0, turns, some, 0)
        at = at + turns * steps


def stats_kernel(
    place_ref,
    table_ref,
    kv_ref,
    other_ref,
    q_in_ref,
    g_in_ref,
    q_ref,
    g_ref,
    out_ref,
    top_ref,
    total_ref,
    weighted_ref,
):
    lay_out(other_ref, q_ref, g_ref, 1 - place_ref[1])
    top_ref[...] = jnp.full_like(top_ref, NEG_FILL)
    total_ref[...] = jnp.zeros_like(total_ref)
    weighted_ref[...] = jnp.zeros_like(weighted_ref)

    def one_step(step):
        slot, spans, keys, query, grad, scores, products = load_step(
            table_ref, kv_ref, q_ref, g_ref, step
        )
        chunk = table_ref[CHUNK + step]
        top = jnp.max(scores, axis=0, keepdims=True)
        weights = jnp.exp2(scores - top)
        row = pl.ds(slot, 1)
        top_ref[chunk, row, :] = top
        total_ref[chunk, row, :] = jnp.sum(weights, axis=0, keepdims=True)
        weighted_ref[chunk, row, :] = jnp.sum(weights * products, axis=0, keepdims=True)

    run_steps(table_ref, one_step)
    parts = range(CHUNKS)
    top = functools.reduce(jnp.maximum, [top_ref[c] for c in parts])
    shares = [jnp.exp2(top_ref[c] - top) for c in parts]
    out_ref[0:8] = top
    out_ref[8:16] = sum(total_ref[c] * shares[c] for c in parts)
    out_ref[16:24] = sum(weighted_ref[c] * shares[c] for c in parts)


def step_gradients(table_ref, kv_ref, q_ref, g_ref, rows_ref, step):
    slot, spans, keys, query, grad, scores, products = load_step(
        table_ref, kv_ref, q_ref, g_ref, step
    )
    probs = jnp.exp2(scores - rows_ref[pl.ds(slot, 1), :])
    score_grad = (probs * (products - rows_ref[pl.ds(8 + slot, 1), :])).astype(jnp.bfloat16)
    return slot, spans, keys, query, grad, probs, score_grad


def key_value_kernel(table_ref, kv_ref, q_ref, g_ref, stats_ref, dkv_ref, rows_ref, acc_ref):
    parts = range(stats_ref.shape[0])
    top = functools.reduce(jnp.maximum, [stats_ref[p, 0:8] for p in parts])
    shares = [jnp.exp2(stats_ref[p, 0:8] - top) for p in parts]
    total = sum(stats_ref[p, 8:16] * shares[p] for p in parts)
    rows_ref[0:8] = top + jnp.log2(total)
    rows_ref[8:16] = sum(stats_ref[p, 16:24] * shares[p] for p in parts) / total
    acc_ref[...] = jnp.zeros_like(acc_ref)

    def one_step(step):
        slot, spans, keys, query, grad, probs, score_grad = step_gradients(
            table_ref, kv_ref, q_ref, g_ref, rows_ref, step
        )
        dk = dot(score_grad, query, NN)
        dv = dot(probs.astype(jnp.bfloat16), grad, NN)
        for n in range(GROUP):
            acc_ref[spans[n]] += dk[n * SPAN : (n + 1) * SPAN]
            acc_ref[spans[n] + 2] += dv[n * SPAN : (n + 1) * SPAN]

    run_steps(table_ref, one_step)
    for n in range(2 * KEYS):
        scaling = SCALING if n % 4 < 2 else 1.0
        dkv_ref[n] = (acc_ref[n] * scaling).astype(jnp.bfloat16)


def near_kernel(
    place_ref, table_ref, kv_ref, q_ref, g_ref, rows_ref, acc_ref, log_ref, delta_ref
):
    acc_ref[...] = jnp.zeros_like(acc_ref)
    for n in range(SLOTS // 2):
        slot = n // 2 * 4 + place_ref[2] * 2 + n % 2
        log_ref[n] = jnp.broadcast_to(rows_ref[pl.ds(slot, 1), :], (HEAD, ROWS)).T
        delta_ref[n] = jnp.broadcast_to(rows_ref[pl.ds(8 + slot, 1), :], (HEAD, ROWS)).T
    add_query_gradients(table_ref, kv_ref, q_ref, g_ref, log_ref, delta_ref, acc_ref)


def add_query_gradients(table_ref, kv_ref, q_ref, g_ref, log_ref, delta_ref, acc_ref):
    def one_step(step):
        slot, own = table_ref[SLOT + step], table_ref[CHUNK + step]
        base = table_ref[BASE + step]
        spans, keys, values = load_keys(table_ref, kv_ref, step)
        query_pos = base + lax.broadcasted_iota(jnp.int32, (SPAN, HEAD), 0)
        first = start_of([table_ref[1 + n] for n in range(3)], query_pos)
        lane = lax.broadcasted_iota(jnp.int32, (1, HEAD), 1)
        raw = dot(q_ref[slot], keys, NT)
        products = dot(g_ref[slot], values, NT)
        log_total, delta = log_ref[own], delta_ref[own]
        parts = []
        for n in range(GROUP // 2):
            low, high = (table_ref[PLACES + step * GROUP + 2 * n + i] for i in range(2))
            pos = jnp.where(lane < SPAN, low, high) + lane % SPAN
            visible = (pos <= query_pos) & (pos >= first)
            cols = slice(n * HEAD, (n + 1) * HEAD)
            scores = raw[:, cols].reshape(HEADS, SPAN, HEAD) * (SCALING * LOG2E)
            scores = jnp.where(visible[None], scores, NEG_FILL).reshape(ROWS, HEAD)
            probs = jnp.exp2(scores - log_total)
            parts.append((probs * (products[:, cols] - delta)).astype(jnp.bfloat16))
        acc_ref[own] += dot(jnp.concatenate(parts, axis=1), keys, NN)

    run_steps(table_ref, one_step)


def far_kernel(
    place_ref, table_ref, kv_ref, q_ref, g_ref, sum_ref, log_ref, delta_ref, out_ref, acc_ref
):
    acc_ref[...] = sum_ref[...]
    add_query_gradients(table_ref, kv_ref, q_ref, g_ref, log_ref, delta_ref, acc_ref)
    xl = place_ref[1]
    for rel in range(2):
        chip = xl if rel == 0 else 1 - xl
        for half in range(2):
            for h in range(HEADS):
                block = acc_ref[chip * 2 + half, h * SPAN : (h + 1) * SPAN, :] * SCALING
                rows, cols = slice(half * SPAN, (half + 1) * SPAN), slice(h * HEAD, (h + 1) * HEAD)
                out_ref[rel, rows, cols] = block.astype(jnp.bfloat16)


def swap(block, axis):
    return lax.ppermute(block, axis, [(0, 1), (1, 0)])


def call(kernel, name, out_shape, in_specs, out_specs, scratch=(), aliases={}):
    return pl.pallas_call(
        kernel,
        out_shape=out_shape,
        in_specs=in_specs,
        out_specs=out_specs,
        scratch_shapes=scratch,
        input_output_aliases=aliases,
        compiler_params=pltpu.CompilerParams(vmem_limit_bytes=40 * 1024 * 1024),
        name=name,
    )


SMEM = pl.BlockSpec(memory_space=pltpu.SMEM)
VMEM = pl.BlockSpec(memory_space=pltpu.VMEM)


KEYS_VALUES = (2 * KEYS, SPAN, HEAD)
LAID_OUT = jax.ShapeDtypeStruct((SLOTS, ROWS, HEAD), jnp.bfloat16)


def prepare(order, place, episodes, own):
    return call(
        prepare_kernel,
        "prepare",
        (*[jax.ShapeDtypeStruct((TABLE,), jnp.int32)] * 3, LAID_OUT, LAID_OUT),
        [SMEM, SMEM, VMEM, VMEM],
        (SMEM, SMEM, SMEM, VMEM, VMEM),
    )(order, place, episodes, own)


def row_stats(place, table, kv_all, other, q, g):
    return call(
        stats_kernel,
        "row_stats",
        (LAID_OUT, LAID_OUT, jax.ShapeDtypeStruct((24, ROWS), jnp.float32)),
        [SMEM, SMEM, VMEM, VMEM, VMEM, VMEM],
        (VMEM, VMEM, VMEM),
        [pltpu.VMEM((CHUNKS, SLOTS, ROWS), jnp.float32)] * 3,
        {4: 0, 5: 1},
    )(place, table, kv_all, other, q, g)


def key_value_gradients(table, kv_all, q, g, stats_all):
    return call(
        key_value_kernel,
        "key_value_gradients",
        (
            jax.ShapeDtypeStruct(KEYS_VALUES, jnp.bfloat16),
            jax.ShapeDtypeStruct((16, ROWS), jnp.float32),
        ),
        [SMEM, VMEM, VMEM, VMEM, VMEM],
        (VMEM, VMEM),
        [pltpu.VMEM(KEYS_VALUES, jnp.float32)],
    )(table, kv_all, q, g, stats_all)


OWN_ROWS = (SLOTS // 2, ROWS, HEAD)


def near_query_gradients(place, table, kv, q, g, rows):
    return call(
        near_kernel,
        "near_query_gradients",
        [jax.ShapeDtypeStruct(OWN_ROWS, jnp.float32)] * 3,
        [SMEM, SMEM, VMEM, VMEM, VMEM, VMEM],
        [VMEM] * 3,
    )(place, table, kv, q, g, rows)


def far_query_gradients(place, table, kv, q, g, near):
    return call(
        far_kernel,
        "far_query_gradients",
        jax.ShapeDtypeStruct((2, 2 * SPAN, HEADS * HEAD), jnp.bfloat16),
        [SMEM, SMEM, VMEM, VMEM, VMEM, VMEM, VMEM, VMEM],
        VMEM,
        [pltpu.VMEM(OWN_ROWS, jnp.float32)],
    )(place, table, kv, q, g, *near)


def per_device(query_rows, key_rows, stored_value_rows, output_grad, span_order, episode_ids):
    tokens = query_rows.shape[1]
    ring = lax.axis_size("y")
    place = jnp.stack([lax.axis_index("y"), lax.axis_index("xl"), lax.axis_index("core")]).astype(
        jnp.int32
    )
    part = lax.broadcasted_iota(jnp.int32, (ring, 2, tokens, HEAD), 1)
    kv = jnp.where(part == 0, key_rows[None], stored_value_rows[None])
    kv_all = lax.all_to_all(kv, "y", 0, 0, tiled=True).reshape(KEYS_VALUES)
    both = jnp.concatenate([query_rows[0], output_grad[0]], axis=1)
    remote = swap(both, "xl")
    own = lax.all_gather(both, "core", axis=0, tiled=True)
    other = lax.all_gather(remote, "core", axis=0, tiled=True)
    table, near_table, far_table, q, g = prepare(span_order, place, episode_ids, own)
    q, g, stats = row_stats(place, table, kv_all, other, q, g)
    stats_all = lax.all_gather(stats, ("xl", "core"), axis=0)
    dkv, rows = key_value_gradients(table, kv_all, q, g, stats_all)
    dkv_parts = lax.all_to_all(dkv.reshape(ring, 2 * tokens, HEAD), "y", 0, 0, tiled=True)
    kv_late, unused = lax.optimization_barrier((kv_all, dkv))
    kv_far = swap(kv_late, "core")
    near = near_query_gradients(place, near_table, kv_late, q, g, rows)
    parts = far_query_gradients(place, far_table, kv_far, q, g, near)
    across = lax.ppermute(parts[1], ("section", "xl"), [(0, 3), (1, 2), (2, 1), (3, 0)])
    straight = swap(parts[0], "section")
    dkv_sum = jnp.sum(dkv_parts.astype(jnp.float32), axis=0).astype(jnp.bfloat16)
    both_dkv = lax.all_gather(dkv_sum, "section", axis=0)
    dkv_back = lax.dynamic_slice_in_dim(both_dkv, 1 - lax.axis_index("section"), 1, 0)
    dk_back, dv_back = dkv_back[:, :tokens], dkv_back[:, tokens:]
    straight, across, dk_back, dv_back = lax.optimization_barrier(
        (straight, across, dk_back, dv_back)
    )
    dq_back = (straight.astype(jnp.float32) + across.astype(jnp.float32)).astype(jnp.bfloat16)
    return (dq_back[None], dk_back, dv_back)


def solution(mesh):
    devices = mesh.devices
    fine = Mesh(
        devices.reshape(devices.shape[0], devices.shape[1], devices.shape[2] // 4, 2, 2),
        ("section", "tp", "y", "xl", "core"),
    )
    rows = P("section", ("y", "xl", "core"), "tp")
    return jax.shard_map(
        per_device,
        mesh=fine,
        in_specs=(rows, rows, rows, rows, P(), P("section", None)),
        out_specs=(rows, rows, rows),
        check_vma=False,
    )
```

```python
import functools

import jax
import jax.numpy as jnp
from jax import lax
from jax.experimental import pallas as pl
from jax.experimental.pallas import tpu as pltpu
from jax.sharding import Mesh
from jax.sharding import PartitionSpec as P

HEAD = 128
SPAN = 64
HEADS = 6
ROWS = HEADS * SPAN
SLOTS = 8
KEYS = 16
GROUP = 4
QUERY_UNROLLS = (4, 2, 1)
UNROLLS = (8, 4, 2, 1)
CHUNKS = KEYS // GROUP
STEPS = SLOTS * CHUNKS + 2 * CHUNKS
SCALING = HEAD ** (-0.5)
LOG2E = 1.4426950408889634
NEG_FILL = -1e30
FAR = 1 << 20
NT = (((1,), (1,)), ((), ()))
NN = (((1,), (0,)), ((), ()))

SLOT = 16
CHUNK = SLOT + STEPS
BASE = CHUNK + STEPS
SPANS = BASE + STEPS
PLACES = SPANS + STEPS * GROUP
TABLE = PLACES + STEPS * GROUP


def dot(a, b, dims):
    return lax.dot_general(a, b, dims, preferred_element_type=jnp.float32)


def start_of(starts, pos):
    first = jnp.zeros_like(pos)
    for s in starts:
        first = jnp.maximum(first, jnp.where(s <= pos, s, 0))
    return first


def list_span(table_ref, starts, step, slot, base, keys, chunk):
    first = start_of(starts, base)
    at = step * GROUP
    for number, place in keys:
        table_ref[SPANS + at] = number
        table_ref[PLACES + at] = place
        seen = (place <= base) & (place + (SPAN - 1) >= first)
        at = at + seen.astype(jnp.int32)
    count = (at - step * GROUP + GROUP - 1) // GROUP
    for extra in range(GROUP):
        table_ref[SPANS + at + extra] = 0
        table_ref[PLACES + at + extra] = FAR
    for c in range(len(keys) // GROUP):
        table_ref[SLOT + step + c] = slot
        table_ref[CHUNK + step + c] = c if chunk is None else chunk
        table_ref[BASE + step + c] = base
    return step + count


def prepare_kernel(
    order_ref, place_ref, episode_ref, own_ref, table_ref, near_ref, far_ref, q_ref, g_ref
):
    y, xl, core = place_ref[0], place_ref[1], place_ref[2]
    ids = episode_ref[...]
    starts = [jnp.sum((ids < v).astype(jnp.int32)) for v in (1, 2, 3)]
    for n, s in enumerate(starts):
        for ref in (table_ref, near_ref, far_ref):
            ref[1 + n] = s

    def keys_of(side):
        return [
            ((k // 2) * 4 + k % 2, order_ref[((k // 2) * 4 + xl * 2 + side) * 2 + k % 2] * SPAN)
            for k in range(KEYS)
        ]

    keys = keys_of(core)

    def list_slot(slot, step):
        base = order_ref[y * SLOTS + slot] * SPAN
        return list_span(table_ref, starts, step, slot, base, keys, None)

    table_ref[0] = lax.fori_loop(0, SLOTS, list_slot, jnp.int32(0))
    for ref, some_keys in ((near_ref, keys), (far_ref, keys_of(1 - core))):

        def list_own_slot(n, step, ref=ref, some_keys=some_keys):
            slot = n // 2 * 4 + core * 2 + n % 2
            base = order_ref[y * SLOTS + slot] * SPAN
            return list_span(ref, starts, step, slot, base, some_keys, n)

        ref[0] = lax.fori_loop(0, SLOTS // 2, list_own_slot, jnp.int32(0))
    lay_out(own_ref, q_ref, g_ref, xl)


def lay_out(ref, q_ref, g_ref, chip):
    for n, out_ref in enumerate((q_ref, g_ref)):
        for i in range(SLOTS // 2):
            for h in range(HEADS):
                out_ref[chip * 4 + i, h * SPAN : (h + 1) * SPAN, :] = ref[
                    i * SPAN : (i + 1) * SPAN, (n * HEADS + h) * HEAD : (n * HEADS + h + 1) * HEAD
                ]


def load_keys(table_ref, kv_ref, step):
    spans = [table_ref[SPANS + step * GROUP + i] for i in range(GROUP)]
    keys = jnp.concatenate([kv_ref[s] for s in spans], axis=0)
    values = jnp.concatenate([kv_ref[s + 2] for s in spans], axis=0)
    return spans, keys, values


def load_step(table_ref, kv_ref, q_ref, g_ref, step):
    slot, base = table_ref[SLOT + step], table_ref[BASE + step]
    spans, keys, values = load_keys(table_ref, kv_ref, step)
    iota = lax.broadcasted_iota(jnp.int32, (SPAN, HEAD), 0)
    pos = jnp.concatenate(
        [table_ref[PLACES + step * GROUP + i] + iota for i in range(GROUP)], axis=0
    )
    query_pos = base + lax.broadcasted_iota(jnp.int32, (1, HEAD), 1) % SPAN
    first = start_of([table_ref[1 + n] for n in range(3)], query_pos)
    visible = (pos <= query_pos) & (pos >= first)
    query, grad = q_ref[slot], g_ref[slot]
    raw = dot(keys, query, NT)
    scores = jnp.concatenate(
        [
            jnp.where(visible, raw[:, g * HEAD : (g + 1) * HEAD] * (SCALING * LOG2E), NEG_FILL)
            for g in range(ROWS // HEAD)
        ],
        axis=1,
    )
    return slot, spans, keys, query, grad, scores, dot(values, grad, NT)


def run_steps(table_ref, one_step, unrolls=UNROLLS):
    at, count = jnp.int32(0), table_ref[0]
    for steps in unrolls:

        def some(n, unused, at=at, steps=steps):
            for i in range(steps):
                one_step(at + n * steps + i)
            return unused

        turns = (count - at) // steps
        lax.fori_loop(0, turns, some, 0)
        at = at + turns * steps


def stats_kernel(
    place_ref,
    table_ref,
    kv_ref,
    other_ref,
    q_in_ref,
    g_in_ref,
    q_ref,
    g_ref,
    out_ref,
    top_ref,
    total_ref,
    weighted_ref,
):
    lay_out(other_ref, q_ref, g_ref, 1 - place_ref[1])
    top_ref[...] = jnp.full_like(top_ref, NEG_FILL)
    total_ref[...] = jnp.zeros_like(total_ref)
    weighted_ref[...] = jnp.zeros_like(weighted_ref)

    def one_step(step):
        slot, spans, keys, query, grad, scores, products = load_step(
            table_ref, kv_ref, q_ref, g_ref, step
        )
        chunk = table_ref[CHUNK + step]
        top = jnp.max(scores, axis=0, keepdims=True)
        weights = jnp.exp2(scores - top)
        row = pl.ds(slot, 1)
        top_ref[chunk, row, :] = top
        total_ref[chunk, row, :] = jnp.sum(weights, axis=0, keepdims=True)
        weighted_ref[chunk, row, :] = jnp.sum(weights * products, axis=0, keepdims=True)

    run_steps(table_ref, one_step)
    parts = range(CHUNKS)
    top = functools.reduce(jnp.maximum, [top_ref[c] for c in parts])
    shares = [jnp.exp2(top_ref[c] - top) for c in parts]
    out_ref[0:8] = top
    out_ref[8:16] = sum(total_ref[c] * shares[c] for c in parts)
    out_ref[16:24] = sum(weighted_ref[c] * shares[c] for c in parts)


def step_gradients(table_ref, kv_ref, q_ref, g_ref, rows_ref, step):
    slot, spans, keys, query, grad, scores, products = load_step(
        table_ref, kv_ref, q_ref, g_ref, step
    )
    probs = jnp.exp2(scores - rows_ref[pl.ds(slot, 1), :])
    score_grad = (probs * (products - rows_ref[pl.ds(8 + slot, 1), :])).astype(jnp.bfloat16)
    return slot, spans, keys, query, grad, probs, score_grad


def key_value_kernel(table_ref, kv_ref, q_ref, g_ref, stats_ref, dkv_ref, rows_ref, acc_ref):
    parts = range(stats_ref.shape[0])
    top = functools.reduce(jnp.maximum, [stats_ref[p, 0:8] for p in parts])
    shares = [jnp.exp2(stats_ref[p, 0:8] - top) for p in parts]
    total = sum(stats_ref[p, 8:16] * shares[p] for p in parts)
    rows_ref[0:8] = top + jnp.log2(total)
    rows_ref[8:16] = sum(stats_ref[p, 16:24] * shares[p] for p in parts) / total
    acc_ref[...] = jnp.zeros_like(acc_ref)

    def one_step(step):
        slot, spans, keys, query, grad, probs, score_grad = step_gradients(
            table_ref, kv_ref, q_ref, g_ref, rows_ref, step
        )
        dk = dot(score_grad, query, NN)
        dv = dot(probs.astype(jnp.bfloat16), grad, NN)
        for n in range(GROUP):
            acc_ref[spans[n]] += dk[n * SPAN : (n + 1) * SPAN]
            acc_ref[spans[n] + 2] += dv[n * SPAN : (n + 1) * SPAN]

    run_steps(table_ref, one_step)
    for n in range(2 * KEYS):
        scaling = SCALING if n % 4 < 2 else 1.0
        dkv_ref[n] = (acc_ref[n] * scaling).astype(jnp.bfloat16)


def near_kernel(
    place_ref, table_ref, kv_ref, q_ref, g_ref, rows_ref, acc_ref, log_ref, delta_ref
):
    acc_ref[...] = jnp.zeros_like(acc_ref)
    for n in range(SLOTS // 2):
        slot = n // 2 * 4 + place_ref[2] * 2 + n % 2
        log_ref[n] = jnp.broadcast_to(rows_ref[pl.ds(slot, 1), :], (HEAD, ROWS)).T
        delta_ref[n] = jnp.broadcast_to(rows_ref[pl.ds(8 + slot, 1), :], (HEAD, ROWS)).T
    add_query_gradients(table_ref, kv_ref, q_ref, g_ref, log_ref, delta_ref, acc_ref)


def add_query_gradients(table_ref, kv_ref, q_ref, g_ref, log_ref, delta_ref, acc_ref):
    def one_step(step):
        slot, own = table_ref[SLOT + step], table_ref[CHUNK + step]
        base = table_ref[BASE + step]
        spans, keys, values = load_keys(table_ref, kv_ref, step)
        query_pos = base + lax.broadcasted_iota(jnp.int32, (SPAN, HEAD), 0)
        first = start_of([table_ref[1 + n] for n in range(3)], query_pos)
        lane = lax.broadcasted_iota(jnp.int32, (1, HEAD), 1)
        raw = dot(q_ref[slot], keys, NT)
        products = dot(g_ref[slot], values, NT)
        log_total, delta = log_ref[own], delta_ref[own]
        parts = []
        for n in range(GROUP // 2):
            low, high = (table_ref[PLACES + step * GROUP + 2 * n + i] for i in range(2))
            pos = jnp.where(lane < SPAN, low, high) + lane % SPAN
            visible = (pos <= query_pos) & (pos >= first)
            cols = slice(n * HEAD, (n + 1) * HEAD)
            scores = raw[:, cols].reshape(HEADS, SPAN, HEAD) * (SCALING * LOG2E)
            scores = jnp.where(visible[None], scores, NEG_FILL).reshape(ROWS, HEAD)
            probs = jnp.exp2(scores - log_total)
            parts.append((probs * (products[:, cols] - delta)).astype(jnp.bfloat16))
        acc_ref[own] += dot(jnp.concatenate(parts, axis=1), keys, NN)

    run_steps(table_ref, one_step, QUERY_UNROLLS)


def far_kernel(
    place_ref, table_ref, kv_ref, q_ref, g_ref, sum_ref, log_ref, delta_ref, out_ref, acc_ref
):
    acc_ref[...] = sum_ref[...]
    add_query_gradients(table_ref, kv_ref, q_ref, g_ref, log_ref, delta_ref, acc_ref)
    xl = place_ref[1]
    for rel in range(2):
        chip = xl if rel == 0 else 1 - xl
        for half in range(2):
            for h in range(HEADS):
                block = acc_ref[chip * 2 + half, h * SPAN : (h + 1) * SPAN, :] * SCALING
                rows, cols = slice(half * SPAN, (half + 1) * SPAN), slice(h * HEAD, (h + 1) * HEAD)
                out_ref[rel, rows, cols] = block.astype(jnp.bfloat16)


def swap(block, axis):
    return lax.ppermute(block, axis, [(0, 1), (1, 0)])


def call(kernel, name, out_shape, in_specs, out_specs, scratch=(), aliases={}):
    return pl.pallas_call(
        kernel,
        out_shape=out_shape,
        in_specs=in_specs,
        out_specs=out_specs,
        scratch_shapes=scratch,
        input_output_aliases=aliases,
        compiler_params=pltpu.CompilerParams(vmem_limit_bytes=40 * 1024 * 1024),
        name=name,
    )


SMEM = pl.BlockSpec(memory_space=pltpu.SMEM)
VMEM = pl.BlockSpec(memory_space=pltpu.VMEM)


KEYS_VALUES = (2 * KEYS, SPAN, HEAD)
LAID_OUT = jax.ShapeDtypeStruct((SLOTS, ROWS, HEAD), jnp.bfloat16)


def prepare(order, place, episodes, own):
    return call(
        prepare_kernel,
        "prepare",
        (*[jax.ShapeDtypeStruct((TABLE,), jnp.int32)] * 3, LAID_OUT, LAID_OUT),
        [SMEM, SMEM, VMEM, VMEM],
        (SMEM, SMEM, SMEM, VMEM, VMEM),
    )(order, place, episodes, own)


def row_stats(place, table, kv_all, other, q, g):
    return call(
        stats_kernel,
        "row_stats",
        (LAID_OUT, LAID_OUT, jax.ShapeDtypeStruct((24, ROWS), jnp.float32)),
        [SMEM, SMEM, VMEM, VMEM, VMEM, VMEM],
        (VMEM, VMEM, VMEM),
        [pltpu.VMEM((CHUNKS, SLOTS, ROWS), jnp.float32)] * 3,
        {4: 0, 5: 1},
    )(place, table, kv_all, other, q, g)


def key_value_gradients(table, kv_all, q, g, stats_all):
    return call(
        key_value_kernel,
        "key_value_gradients",
        (
            jax.ShapeDtypeStruct(KEYS_VALUES, jnp.bfloat16),
            jax.ShapeDtypeStruct((16, ROWS), jnp.float32),
        ),
        [SMEM, VMEM, VMEM, VMEM, VMEM],
        (VMEM, VMEM),
        [pltpu.VMEM(KEYS_VALUES, jnp.float32)],
    )(table, kv_all, q, g, stats_all)


OWN_ROWS = (SLOTS // 2, ROWS, HEAD)


def near_query_gradients(place, table, kv, q, g, rows):
    return call(
        near_kernel,
        "near_query_gradients",
        [jax.ShapeDtypeStruct(OWN_ROWS, jnp.float32)] * 3,
        [SMEM, SMEM, VMEM, VMEM, VMEM, VMEM],
        [VMEM] * 3,
    )(place, table, kv, q, g, rows)


def far_query_gradients(place, table, kv, q, g, near):
    return call(
        far_kernel,
        "far_query_gradients",
        jax.ShapeDtypeStruct((2, 2 * SPAN, HEADS * HEAD), jnp.bfloat16),
        [SMEM, SMEM, VMEM, VMEM, VMEM, VMEM, VMEM, VMEM],
        VMEM,
        [pltpu.VMEM(OWN_ROWS, jnp.float32)],
    )(place, table, kv, q, g, *near)


def per_device(query_rows, key_rows, stored_value_rows, output_grad, span_order, episode_ids):
    tokens = query_rows.shape[1]
    ring = lax.axis_size("y")
    place = jnp.stack([lax.axis_index("y"), lax.axis_index("xl"), lax.axis_index("core")]).astype(
        jnp.int32
    )
    part = lax.broadcasted_iota(jnp.int32, (ring, 2, tokens, HEAD), 1)
    kv = jnp.where(part == 0, key_rows[None], stored_value_rows[None])
    kv_all = lax.all_to_all(kv, "y", 0, 0, tiled=True).reshape(KEYS_VALUES)
    both = jnp.concatenate([query_rows[0], output_grad[0]], axis=1)
    remote = swap(both, "xl")
    own = lax.all_gather(both, "core", axis=0, tiled=True)
    other = lax.all_gather(remote, "core", axis=0, tiled=True)
    table, near_table, far_table, q, g = prepare(span_order, place, episode_ids, own)
    q, g, stats = row_stats(place, table, kv_all, other, q, g)
    stats_all = lax.all_gather(stats, ("xl", "core"), axis=0)
    dkv, rows = key_value_gradients(table, kv_all, q, g, stats_all)
    dkv_parts = lax.all_to_all(dkv.reshape(ring, 2 * tokens, HEAD), "y", 0, 0, tiled=True)
    kv_late, unused = lax.optimization_barrier((kv_all, dkv))
    kv_far = swap(kv_late, "core")
    near = near_query_gradients(place, near_table, kv_late, q, g, rows)
    parts = far_query_gradients(place, far_table, kv_far, q, g, near)
    across = lax.ppermute(parts[1], ("section", "xl"), [(0, 3), (1, 2), (2, 1), (3, 0)])
    straight = swap(parts[0], "section")
    dkv_sum = jnp.sum(dkv_parts.astype(jnp.float32), axis=0).astype(jnp.bfloat16)
    both_dkv = lax.all_gather(dkv_sum, "section", axis=0)
    dkv_back = lax.dynamic_slice_in_dim(both_dkv, 1 - lax.axis_index("section"), 1, 0)
    dk_back, dv_back = dkv_back[:, :tokens], dkv_back[:, tokens:]
    straight, across, dk_back, dv_back = lax.optimization_barrier(
        (straight, across, dk_back, dv_back)
    )
    dq_back = (straight.astype(jnp.float32) + across.astype(jnp.float32)).astype(jnp.bfloat16)
    return (dq_back[None], dk_back, dv_back)


def solution(mesh):
    devices = mesh.devices
    fine = Mesh(
        devices.reshape(devices.shape[0], devices.shape[1], devices.shape[2] // 4, 2, 2),
        ("section", "tp", "y", "xl", "core"),
    )
    rows = P("section", ("y", "xl", "core"), "tp")
    return jax.shard_map(
        per_device,
        mesh=fine,
        in_specs=(rows, rows, rows, rows, P(), P("section", None)),
        out_specs=(rows, rows, rows),
        check_vma=False,
    )
```

```python
import functools

import jax
import jax.numpy as jnp
from jax import lax
from jax.experimental import pallas as pl
from jax.experimental.pallas import tpu as pltpu
from jax.sharding import Mesh
from jax.sharding import PartitionSpec as P

HEAD = 128
SPAN = 64
HEADS = 6
ROWS = HEADS * SPAN
SLOTS = 8
KEYS = 16
GROUP = 4
QUERY_UNROLLS = (4, 2, 1)
UNROLLS = (8, 4, 2, 1)
CHUNKS = KEYS // GROUP
STEPS = SLOTS * CHUNKS + 2 * CHUNKS
SCALING = HEAD ** (-0.5)
LOG2E = 1.4426950408889634
NEG_FILL = -1e30
FAR = 1 << 20
NT = (((1,), (1,)), ((), ()))
NN = (((1,), (0,)), ((), ()))

SLOT = 16
CHUNK = SLOT + STEPS
BASE = CHUNK + STEPS
SPANS = BASE + STEPS
PLACES = SPANS + STEPS * GROUP
TABLE = PLACES + STEPS * GROUP


def dot(a, b, dims):
    return lax.dot_general(a, b, dims, preferred_element_type=jnp.float32)


def start_of(starts, pos):
    first = jnp.zeros_like(pos)
    for s in starts:
        first = jnp.maximum(first, jnp.where(s <= pos, s, 0))
    return first


def list_span(table_ref, starts, step, slot, base, keys, chunk):
    first = start_of(starts, base)
    at = step * GROUP
    for number, place in keys:
        table_ref[SPANS + at] = number
        table_ref[PLACES + at] = place
        seen = (place <= base) & (place + (SPAN - 1) >= first)
        at = at + seen.astype(jnp.int32)
    count = (at - step * GROUP + GROUP - 1) // GROUP
    for extra in range(GROUP):
        table_ref[SPANS + at + extra] = 0
        table_ref[PLACES + at + extra] = FAR
    for c in range(len(keys) // GROUP):
        table_ref[SLOT + step + c] = slot
        table_ref[CHUNK + step + c] = c if chunk is None else chunk
        table_ref[BASE + step + c] = base
    return step + count


def prepare_kernel(
    order_ref, place_ref, episode_ref, own_ref, table_ref, near_ref, far_ref, q_ref, g_ref
):
    y, xl, core = place_ref[0], place_ref[1], place_ref[2]
    ids = episode_ref[...]
    starts = [jnp.sum((ids < v).astype(jnp.int32)) for v in (1, 2, 3)]
    for n, s in enumerate(starts):
        for ref in (table_ref, near_ref, far_ref):
            ref[1 + n] = s

    def keys_of(side):
        return [
            ((k // 2) * 4 + k % 2, order_ref[((k // 2) * 4 + xl * 2 + side) * 2 + k % 2] * SPAN)
            for k in range(KEYS)
        ]

    keys = keys_of(core)

    def list_slot(slot, step):
        base = order_ref[y * SLOTS + slot] * SPAN
        return list_span(table_ref, starts, step, slot, base, keys, None)

    table_ref[0] = lax.fori_loop(0, SLOTS, list_slot, jnp.int32(0))
    for ref, some_keys in ((near_ref, keys), (far_ref, keys_of(1 - core))):

        def list_own_slot(n, step, ref=ref, some_keys=some_keys):
            slot = n // 2 * 4 + core * 2 + n % 2
            base = order_ref[y * SLOTS + slot] * SPAN
            return list_span(ref, starts, step, slot, base, some_keys, n)

        ref[0] = lax.fori_loop(0, SLOTS // 2, list_own_slot, jnp.int32(0))
    lay_out(own_ref, q_ref, g_ref, xl)


def lay_out(ref, q_ref, g_ref, chip):
    for n, out_ref in enumerate((q_ref, g_ref)):
        for i in range(SLOTS // 2):
            for h in range(HEADS):
                out_ref[chip * 4 + i, h * SPAN : (h + 1) * SPAN, :] = ref[
                    i * SPAN : (i + 1) * SPAN, (n * HEADS + h) * HEAD : (n * HEADS + h + 1) * HEAD
                ]


def load_keys(table_ref, kv_ref, step):
    spans = [table_ref[SPANS + step * GROUP + i] for i in range(GROUP)]
    keys = jnp.concatenate([kv_ref[s] for s in spans], axis=0)
    values = jnp.concatenate([kv_ref[s + 2] for s in spans], axis=0)
    return spans, keys, values


def load_step(table_ref, kv_ref, q_ref, g_ref, step):
    slot, base = table_ref[SLOT + step], table_ref[BASE + step]
    spans, keys, values = load_keys(table_ref, kv_ref, step)
    iota = lax.broadcasted_iota(jnp.int32, (SPAN, HEAD), 0)
    pos = jnp.concatenate(
        [table_ref[PLACES + step * GROUP + i] + iota for i in range(GROUP)], axis=0
    )
    query_pos = base + lax.broadcasted_iota(jnp.int32, (1, HEAD), 1) % SPAN
    first = start_of([table_ref[1 + n] for n in range(3)], query_pos)
    visible = (pos <= query_pos) & (pos >= first)
    query, grad = q_ref[slot], g_ref[slot]
    raw = dot(keys, query, NT)
    scores = jnp.concatenate(
        [
            jnp.where(visible, raw[:, g * HEAD : (g + 1) * HEAD] * (SCALING * LOG2E), NEG_FILL)
            for g in range(ROWS // HEAD)
        ],
        axis=1,
    )
    return slot, spans, keys, query, grad, scores, dot(values, grad, NT)


def run_steps(table_ref, one_step, unrolls=UNROLLS):
    at, count = jnp.int32(0), table_ref[0]
    for steps in unrolls:

        def some(n, unused, at=at, steps=steps):
            for i in range(steps):
                one_step(at + n * steps + i)
            return unused

        turns = (count - at) // steps
        lax.fori_loop(0, turns, some, 0)
        at = at + turns * steps


def stats_kernel(
    place_ref,
    table_ref,
    kv_ref,
    other_ref,
    q_in_ref,
    g_in_ref,
    q_ref,
    g_ref,
    out_ref,
    top_ref,
    total_ref,
    weighted_ref,
):
    lay_out(other_ref, q_ref, g_ref, 1 - place_ref[1])
    top_ref[...] = jnp.full_like(top_ref, NEG_FILL)
    total_ref[...] = jnp.zeros_like(total_ref)
    weighted_ref[...] = jnp.zeros_like(weighted_ref)

    def one_step(step):
        slot, spans, keys, query, grad, scores, products = load_step(
            table_ref, kv_ref, q_ref, g_ref, step
        )
        chunk = table_ref[CHUNK + step]
        top = jnp.max(scores, axis=0, keepdims=True)
        weights = jnp.exp2(scores - top)
        row = pl.ds(slot, 1)
        top_ref[chunk, row, :] = top
        total_ref[chunk, row, :] = jnp.sum(weights, axis=0, keepdims=True)
        weighted_ref[chunk, row, :] = jnp.sum(weights * products, axis=0, keepdims=True)

    run_steps(table_ref, one_step)
    parts = range(CHUNKS)
    top = functools.reduce(jnp.maximum, [top_ref[c] for c in parts])
    shares = [jnp.exp2(top_ref[c] - top) for c in parts]
    out_ref[0:8] = top
    out_ref[8:16] = sum(total_ref[c] * shares[c] for c in parts)
    out_ref[16:24] = sum(weighted_ref[c] * shares[c] for c in parts)


def step_gradients(table_ref, kv_ref, q_ref, g_ref, rows_ref, step):
    slot, spans, keys, query, grad, scores, products = load_step(
        table_ref, kv_ref, q_ref, g_ref, step
    )
    probs = jnp.exp2(scores - rows_ref[pl.ds(slot, 1), :])
    score_grad = (probs * (products - rows_ref[pl.ds(8 + slot, 1), :])).astype(jnp.bfloat16)
    return slot, spans, keys, query, grad, probs, score_grad


def key_value_kernel(table_ref, kv_ref, q_ref, g_ref, stats_ref, dkv_ref, rows_ref, acc_ref):
    parts = range(stats_ref.shape[0])
    top = functools.reduce(jnp.maximum, [stats_ref[p, 0:8] for p in parts])
    shares = [jnp.exp2(stats_ref[p, 0:8] - top) for p in parts]
    total = sum(stats_ref[p, 8:16] * shares[p] for p in parts)
    rows_ref[0:8] = top + jnp.log2(total)
    rows_ref[8:16] = sum(stats_ref[p, 16:24] * shares[p] for p in parts) / total
    acc_ref[...] = jnp.zeros_like(acc_ref)

    def one_step(step):
        slot, spans, keys, query, grad, probs, score_grad = step_gradients(
            table_ref, kv_ref, q_ref, g_ref, rows_ref, step
        )
        dk = dot(score_grad, query, NN)
        dv = dot(probs.astype(jnp.bfloat16), grad, NN)
        for n in range(GROUP):
            acc_ref[spans[n]] += dk[n * SPAN : (n + 1) * SPAN]
            acc_ref[spans[n] + 2] += dv[n * SPAN : (n + 1) * SPAN]

    run_steps(table_ref, one_step)
    for n in range(2 * KEYS):
        scaling = SCALING if n % 4 < 2 else 1.0
        dkv_ref[n] = (acc_ref[n] * scaling).astype(jnp.bfloat16)


def near_kernel(
    place_ref, table_ref, kv_ref, q_ref, g_ref, rows_ref, acc_ref, log_ref, delta_ref
):
    acc_ref[...] = jnp.zeros_like(acc_ref)
    for n in range(SLOTS // 2):
        slot = n // 2 * 4 + place_ref[2] * 2 + n % 2
        log_ref[n] = jnp.broadcast_to(rows_ref[pl.ds(slot, 1), :], (HEAD, ROWS)).T
        delta_ref[n] = jnp.broadcast_to(rows_ref[pl.ds(8 + slot, 1), :], (HEAD, ROWS)).T
    add_query_gradients(table_ref, kv_ref, q_ref, g_ref, log_ref, delta_ref, acc_ref)


def add_query_gradients(table_ref, kv_ref, q_ref, g_ref, log_ref, delta_ref, acc_ref):
    def one_step(step):
        slot, own = table_ref[SLOT + step], table_ref[CHUNK + step]
        base = table_ref[BASE + step]
        spans, keys, values = load_keys(table_ref, kv_ref, step)
        query_pos = base + lax.broadcasted_iota(jnp.int32, (SPAN, HEAD), 0)
        first = start_of([table_ref[1 + n] for n in range(3)], query_pos)
        lane = lax.broadcasted_iota(jnp.int32, (1, HEAD), 1)
        raw = dot(q_ref[slot], keys, NT)
        products = dot(g_ref[slot], values, NT)
        log_total, delta = log_ref[own], delta_ref[own]
        parts = []
        for n in range(GROUP // 2):
            low, high = (table_ref[PLACES + step * GROUP + 2 * n + i] for i in range(2))
            pos = jnp.where(lane < SPAN, low, high) + lane % SPAN
            visible = (pos <= query_pos) & (pos >= first)
            cols = slice(n * HEAD, (n + 1) * HEAD)
            scores = raw[:, cols].reshape(HEADS, SPAN, HEAD) * (SCALING * LOG2E)
            scores = jnp.where(visible[None], scores, NEG_FILL).reshape(ROWS, HEAD)
            probs = jnp.exp2(scores - log_total)
            parts.append((probs * (products[:, cols] - delta)).astype(jnp.bfloat16))
        acc_ref[own] += dot(jnp.concatenate(parts, axis=1), keys, NN)

    run_steps(table_ref, one_step, QUERY_UNROLLS)


def far_kernel(
    place_ref, table_ref, kv_ref, q_ref, g_ref, sum_ref, log_ref, delta_ref, out_ref, acc_ref
):
    acc_ref[...] = sum_ref[...]
    add_query_gradients(table_ref, kv_ref, q_ref, g_ref, log_ref, delta_ref, acc_ref)
    xl = place_ref[1]
    for rel in range(2):
        chip = xl if rel == 0 else 1 - xl
        for half in range(2):
            for h in range(HEADS):
                block = acc_ref[chip * 2 + half, h * SPAN : (h + 1) * SPAN, :] * SCALING
                rows, cols = slice(half * SPAN, (half + 1) * SPAN), slice(h * HEAD, (h + 1) * HEAD)
                out_ref[rel, rows, cols] = block.astype(jnp.bfloat16)


def swap(block, axis):
    return lax.ppermute(block, axis, [(0, 1), (1, 0)])


def call(kernel, name, out_shape, in_specs, out_specs, scratch=(), aliases={}):
    return pl.pallas_call(
        kernel,
        out_shape=out_shape,
        in_specs=in_specs,
        out_specs=out_specs,
        scratch_shapes=scratch,
        input_output_aliases=aliases,
        compiler_params=pltpu.CompilerParams(vmem_limit_bytes=40 * 1024 * 1024),
        name=name,
    )


SMEM = pl.BlockSpec(memory_space=pltpu.SMEM)
VMEM = pl.BlockSpec(memory_space=pltpu.VMEM)


KEYS_VALUES = (2 * KEYS, SPAN, HEAD)
LAID_OUT = jax.ShapeDtypeStruct((SLOTS, ROWS, HEAD), jnp.bfloat16)


def prepare(order, place, episodes, own):
    return call(
        prepare_kernel,
        "prepare",
        (*[jax.ShapeDtypeStruct((TABLE,), jnp.int32)] * 3, LAID_OUT, LAID_OUT),
        [SMEM, SMEM, VMEM, VMEM],
        (SMEM, SMEM, SMEM, VMEM, VMEM),
    )(order, place, episodes, own)


def row_stats(place, table, kv_all, other, q, g):
    return call(
        stats_kernel,
        "row_stats",
        (LAID_OUT, LAID_OUT, jax.ShapeDtypeStruct((24, ROWS), jnp.float32)),
        [SMEM, SMEM, VMEM, VMEM, VMEM, VMEM],
        (VMEM, VMEM, VMEM),
        [pltpu.VMEM((CHUNKS, SLOTS, ROWS), jnp.float32)] * 3,
        {4: 0, 5: 1},
    )(place, table, kv_all, other, q, g)


def key_value_gradients(table, kv_all, q, g, stats_all):
    return call(
        key_value_kernel,
        "key_value_gradients",
        (
            jax.ShapeDtypeStruct(KEYS_VALUES, jnp.bfloat16),
            jax.ShapeDtypeStruct((16, ROWS), jnp.float32),
        ),
        [SMEM, VMEM, VMEM, VMEM, VMEM],
        (VMEM, VMEM),
        [pltpu.VMEM(KEYS_VALUES, jnp.float32)],
    )(table, kv_all, q, g, stats_all)


OWN_ROWS = (SLOTS // 2, ROWS, HEAD)


def near_query_gradients(place, table, kv, q, g, rows):
    return call(
        near_kernel,
        "near_query_gradients",
        [jax.ShapeDtypeStruct(OWN_ROWS, jnp.float32)] * 3,
        [SMEM, SMEM, VMEM, VMEM, VMEM, VMEM],
        [VMEM] * 3,
    )(place, table, kv, q, g, rows)


def far_query_gradients(place, table, kv, q, g, near):
    return call(
        far_kernel,
        "far_query_gradients",
        jax.ShapeDtypeStruct((2, 2 * SPAN, HEADS * HEAD), jnp.bfloat16),
        [SMEM, SMEM, VMEM, VMEM, VMEM, VMEM, VMEM, VMEM],
        VMEM,
        [pltpu.VMEM(OWN_ROWS, jnp.float32)],
    )(place, table, kv, q, g, *near)


def per_device(query_rows, key_rows, stored_value_rows, output_grad, span_order, episode_ids):
    tokens = query_rows.shape[1]
    ring = lax.axis_size("y")
    place = jnp.stack([lax.axis_index("y"), lax.axis_index("xl"), lax.axis_index("core")]).astype(
        jnp.int32
    )
    kv = jnp.concatenate([key_rows, stored_value_rows], axis=1)
    kv = jnp.broadcast_to(kv, (ring, 2 * tokens, HEAD))
    kv_all = lax.all_to_all(kv, "y", 0, 0, tiled=True).reshape(KEYS_VALUES)
    both = jnp.concatenate([query_rows[0], output_grad[0]], axis=1)
    remote = swap(both, "xl")
    own = lax.all_gather(both, "core", axis=0, tiled=True)
    other = lax.all_gather(remote, "core", axis=0, tiled=True)
    table, near_table, far_table, q, g = prepare(span_order, place, episode_ids, own)
    q, g, stats = row_stats(place, table, kv_all, other, q, g)
    stats_all = lax.all_gather(stats, ("xl", "core"), axis=0)
    dkv, rows = key_value_gradients(table, kv_all, q, g, stats_all)
    dkv_parts = lax.all_to_all(dkv.reshape(ring, 2 * tokens, HEAD), "y", 0, 0, tiled=True)
    kv_late, unused = lax.optimization_barrier((kv_all, dkv))
    kv_far = swap(kv_late, "core")
    near = near_query_gradients(place, near_table, kv_late, q, g, rows)
    parts = far_query_gradients(place, far_table, kv_far, q, g, near)
    across = lax.ppermute(parts[1], ("section", "xl"), [(0, 3), (1, 2), (2, 1), (3, 0)])
    straight = swap(parts[0], "section")
    dkv_sum = jnp.sum(dkv_parts.astype(jnp.float32), axis=0).astype(jnp.bfloat16)
    both_dkv = lax.all_gather(dkv_sum, "section", axis=0)
    dkv_back = lax.dynamic_slice_in_dim(both_dkv, 1 - lax.axis_index("section"), 1, 0)
    dk_back, dv_back = dkv_back[:, :tokens], dkv_back[:, tokens:]
    straight, across, dk_back, dv_back = lax.optimization_barrier(
        (straight, across, dk_back, dv_back)
    )
    dq_back = (straight.astype(jnp.float32) + across.astype(jnp.float32)).astype(jnp.bfloat16)
    return (dq_back[None], dk_back, dv_back)


def solution(mesh):
    devices = mesh.devices
    fine = Mesh(
        devices.reshape(devices.shape[0], devices.shape[1], devices.shape[2] // 4, 2, 2),
        ("section", "tp", "y", "xl", "core"),
    )
    rows = P("section", ("y", "xl", "core"), "tp")
    return jax.shard_map(
        per_device,
        mesh=fine,
        in_specs=(rows, rows, rows, rows, P(), P("section", None)),
        out_specs=(rows, rows, rows),
        check_vma=False,
    )
```
